32 devices in a mesh: seg: 4 (over y, core), sec: 8 (over z, x).
Axes of the slice: x: 2, y: 2, z: 4, core: 2. Of those that a mesh axis runs over, the one named last changes fastest.
Arguments:
- theta_in: float32 [4, 16, 128, 128], P('seg', 'sec'), may hold values from -6 to 6
- left_env: float32 [9, 16, 128, 128], P(None, 'sec'), may hold values from -0.0017089844 to 0.0017089844
- site_maps: float32 [4, 16, 128, 128], P('seg', 'sec'), may hold values from -1 to 2, as said below
- right_env: float32 [4, 9, 16, 128, 128], P('seg', None, 'sec'), may hold values from -8 to 8
- mpo_mask: int32 [9, 16], P(None, 'sec'), may hold values 0 or 1
- ranks: int32 [4, 16], P('seg', 'sec'), may hold values from 64 to 128
Outputs:
- theta_out: float32 [4, 16, 128, 128], P('seg', 'sec')
- density: float32 [4, 16, 128, 128], P('seg', 'sec')
The draws below stay inside these ranges and needn't reach their ends.
Inputs may be any that keep to these rules, and one draw needn't show every extreme that they name: `site_maps`: each block of a segment's map is the identity plus a full matrix of entries of size about 1 / (4 sqrt(128)).
All inputs are finite; a program needn't handle non-finite values. No bound on the sum of `mpo_mask` on one device may be relied on, other than what follows from the above.
Results may differ from the reference program's by a relative error of at most 0.0003.
Values sent between devices are 32-bit elements; how exact they have to be, the bound alone decides.
A program may use at most 64 MiB of HBM per device.

```python
import math
import jax
import jax.numpy as jnp
from jax import lax

SB = 128
W = 9
ITERS = 4
NSEG = 4
NSEC = 16


def draw_site_maps(key, part):
    noise = jax.random.normal(key, (NSEG, NSEC, SB, SB), jnp.float32)
    return jnp.eye(SB, dtype=jnp.float32) + 0.25 * noise / math.sqrt(SB)


def draw_right_env(key, part):
    first = jax.random.fold_in(key, 0)
    noise = jax.random.normal(first, (NSEG, W, NSEC, SB, SB), jnp.float32)
    noise = jnp.clip(noise, -5.0, 5.0)
    position = jnp.arange(NSEC, dtype=jnp.float32) / max(NSEC - 1, 1)
    scale = jnp.exp(math.log(3.0) * position)
    return noise * scale[None, None, :, None, None] / math.sqrt(SB)


def with_ends(entries, rng, least, largest):
    dims = entries.shape
    place = [jax.random.randint(jax.random.fold_in(rng, axis), (), 0, dims[axis]) for axis in range(len(dims))]
    entries = entries.at[tuple(place)].set(least)
    longest = dims.index(max(dims))
    place[longest] = (place[longest] + 1) % dims[longest]
    return entries.at[tuple(place)].set(largest)


def shard_levels(rng, dims, cuts, smallest, largest):
    gain, own = 1.0, jax.random.fold_in(rng, 6)
    for dim, blocks in cuts:
        heights = jnp.exp(jax.random.uniform(jax.random.fold_in(own, dim), (blocks,), jnp.float32, smallest / len(cuts), largest / len(cuts)))
        gain = gain * jnp.repeat(heights, dims[dim] // blocks).reshape([-1 if axis == dim else 1 for axis in range(len(dims))])
    return gain


def bell_draw(key, dims, spread, limit, cuts=(), held_as=jnp.bfloat16):
    array = jax.random.normal(key, dims, jnp.float32) * spread
    if len(cuts) > 0:
        array = shard_levels(key, dims, cuts, -0.22, 0.18) * array
    return jnp.clip(array, min=-limit, max=limit).astype(held_as)


def setup_inputs(seed: int = 0) -> dict:
    splits = jax.random.split(jax.random.key(seed), 7)
    return {
        "theta_in": bell_draw(splits[0], (NSEG, NSEC, SB, SB), 1.0, 6.0, ((0, 4), (1, 8)), jnp.float32),
        "left_env": bell_draw(splits[1], (W, NSEC, SB, SB), (90000 * SB) ** -0.5, 0.0017089844, ((1, 8),), jnp.float32),
        "site_maps": draw_site_maps(jax.random.fold_in(splits[6], 71), 0),
        "right_env": draw_right_env(jax.random.fold_in(splits[6], 71), 0),
        "mpo_mask": with_ends((jax.random.randint(splits[4], (W, NSEC), 0, 4) < 3).astype(jnp.int32), jax.random.fold_in(splits[4], 1), 0, 1),
        "ranks": with_ends(jax.random.randint(splits[5], (NSEG, NSEC), SB // 2, SB + 1), jax.random.fold_in(splits[5], 1), SB // 2, SB).astype(jnp.int32),
    }


HIGH = lax.Precision.HIGHEST
EPS = 1e-06

def advance_env(env, maps):
    partial_env = jnp.einsum('wkac,kcd->wkad', env, maps, precision=HIGH)
    return jnp.einsum('kab,wkad->wkbd', maps, partial_env, precision=HIGH)

def shifted_terms(padded, count, blocks):
    pieces = []
    for term in range(count):
        offset = 1 + term % 3 - 1
        pieces.append(padded[term, offset:offset + blocks])
    return jnp.stack(pieces, axis=0)

def reference(theta_in, left_env, site_maps, right_env, mpo_mask, ranks):
    keep_terms = mpo_mask.astype(jnp.float32)[:, :, None, None]
    env = left_env
    vectors = []
    densities = []
    for segment in range(NSEG):
        if segment > 0:
            env = advance_env(env, site_maps[segment - 1])
        vector = theta_in[segment]
        right = right_env[segment]
        weighted = env * keep_terms
        for step in range(ITERS):
            products = jnp.einsum('kab,wkbc->wkac', vector, right, precision=HIGH)
            padded = jnp.pad(products, ((0, 0), (1, 1), (0, 0), (0, 0)))
            gathered = shifted_terms(padded, W, NSEC)
            image = jnp.einsum('wkab,wkbc->kac', weighted, gathered, precision=HIGH)
            total = jnp.sum(image * image)
            vector = image * lax.rsqrt(total / (NSEC * SB * SB) + EPS)
        rows = lax.broadcasted_iota(jnp.int32, (NSEC, SB), 1) < ranks[segment][:, None]
        trimmed = vector * rows.astype(jnp.float32)[:, :, None]
        density = jnp.einsum('kab,kcb->kac', trimmed, trimmed, precision=HIGH) / SB
        vectors.append(vector)
        densities.append(density)
    return (jnp.stack(vectors, axis=0), jnp.stack(densities, axis=0))
```

```python
import functools

import jax
import jax.numpy as jnp
from jax import lax
from jax.experimental import pallas as pl
from jax.experimental.pallas import tpu as pltpu
from jax.sharding import PartitionSpec as P

ITERS = 4
EPS = 1e-06
MESH = pl.DeviceIdType.MESH
F32, BF16 = jnp.float32, jnp.bfloat16


def split(x):
    high = x.astype(BF16)
    low = (x - high.astype(F32)).astype(BF16)
    return high, low


def wide(x):
    return jnp.concatenate(split(x), axis=1)


def twice(x):
    pair = wide(x)
    return jnp.concatenate([pair, pair], axis=0)


def dot(a, b):
    return lax.dot_general(a, b, (((1,), (0,)), ((), ())), preferred_element_type=F32)


def halves(x):
    n = x.shape[1] // 2
    return x[:, :n] + x[:, n:]


def squares(x):
    return jnp.sum((x * x).reshape(-1, 8, x.shape[1]), axis=0)


def kernel(
    n_seg, n_sec, groups, theta, left, maps, right, mask, ranks, theta_out, density,
    lf, rt, mp, amat, rhalo, vh, vs, l2, r2, red,
    local_sem, m_send, m_recv, r_send, r_recv, v_send, v_recv, s_send, s_recv,
):
    seg, sec = lax.axis_index("seg"), lax.axis_index("sec")
    blocks, n = theta.shape[1], theta.shape[2]
    terms = left.shape[0]
    has_low, has_high = sec > 0, sec < n_sec - 1
    row = {}
    start = {}
    for d in (-1, 0, 1):
        start[d] = len(row) * n
        for w in groups[d]:
            row[w] = len(row) * n

    loads = [
        pltpu.make_async_copy(left, lf, local_sem.at[0]),
        pltpu.make_async_copy(right.at[0], rt, local_sem.at[1]),
        pltpu.make_async_copy(theta.at[0], vs.at[0], local_sem.at[2]),
    ]
    for load in loads:
        load.start()

    barrier = pltpu.get_barrier_semaphore()
    for d in range(1, n_seg):
        pl.semaphore_signal(barrier, inc=1, device_id={"seg": lax.rem(seg + d, n_seg)}, device_id_type=MESH)
    for d in range(1, n_sec):
        pl.semaphore_signal(barrier, inc=1, device_id={"sec": lax.rem(sec + d, n_sec)}, device_id_type=MESH)
    pl.semaphore_wait(barrier, n_seg + n_sec - 2)

    def m_copy(d):
        return pltpu.make_async_remote_copy(
            src_ref=maps.at[0], dst_ref=mp.at[seg], send_sem=m_send.at[d - 1], recv_sem=m_recv.at[seg],
            device_id={"seg": seg + d}, device_id_type=MESH,
        )

    def m_arrival(j):
        return pltpu.make_async_remote_copy(
            src_ref=maps.at[0], dst_ref=mp.at[j], send_sem=m_send.at[0], recv_sem=m_recv.at[j],
            device_id={"seg": j}, device_id_type=MESH,
        )

    def v_copy(t, source, side):
        other = sec - 1 if side == 0 else sec + 1
        return pltpu.make_async_remote_copy(
            src_ref=source, dst_ref=vh.at[t, 1 - side], send_sem=v_send.at[t, side],
            recv_sem=v_recv.at[t, 1 - side], device_id={"sec": other}, device_id_type=MESH,
        )

    def v_arrival(t, side):
        other = sec - 1 if side == 0 else sec + 1
        return pltpu.make_async_remote_copy(
            src_ref=vs.at[0, 0], dst_ref=vh.at[t, side], send_sem=v_send.at[t, side],
            recv_sem=v_recv.at[t, side], device_id={"sec": other}, device_id_type=MESH,
        )

    def r_copies(side):
        other = sec - 1 if side == 0 else sec + 1
        q, shift = (0, 1) if side == 0 else (blocks - 1, -1)
        return [
            pltpu.make_async_remote_copy(
                src_ref=right.at[0, w, q], dst_ref=rhalo.at[1 - side, i], send_sem=r_send.at[side, i],
                recv_sem=r_recv.at[1 - side, i], device_id={"sec": other}, device_id_type=MESH,
            )
            for i, w in enumerate(groups[shift])
        ]

    def r_arrivals(side):
        other = sec - 1 if side == 0 else sec + 1
        shift = -1 if side == 0 else 1
        return [
            pltpu.make_async_remote_copy(
                src_ref=right.at[0, w, 0], dst_ref=rhalo.at[side, i], send_sem=r_send.at[side, i],
                recv_sem=r_recv.at[side, i], device_id={"sec": other}, device_id_type=MESH,
            )
            for i, w in enumerate(groups[shift])
        ]

    def s_copy(stage, d):
        return pltpu.make_async_remote_copy(
            src_ref=red.at[stage, sec], dst_ref=red.at[stage, sec], send_sem=s_send.at[stage, d],
            recv_sem=s_recv.at[stage, sec], device_id={"sec": lax.rem(sec + d, n_sec)}, device_id_type=MESH,
        )

    def s_arrival(stage, d):
        other = lax.rem(sec + d, n_sec)
        return pltpu.make_async_remote_copy(
            src_ref=red.at[stage, sec], dst_ref=red.at[stage, other], send_sem=s_send.at[stage, d],
            recv_sem=s_recv.at[stage, other], device_id={"sec": other}, device_id_type=MESH,
        )

    for d in range(1, n_seg):
        @pl.when(seg + d < n_seg)
        def _():
            m_copy(d).start()

    for side, there in ((0, has_low), (1, has_high)):
        q = 0 if side == 0 else blocks - 1
        @pl.when(there)
        def _():
            v_copy(0, theta.at[0, q], side).start()
            for copy in r_copies(side):
                copy.start()

        @pl.when(jnp.logical_not(there))
        def _():
            rhalo[side] = jnp.zeros_like(rhalo[side])
            for t in range(ITERS):
                vh[t, side] = jnp.zeros_like(vh[t, side])

    loads[0].wait()
    for q in range(blocks):
        for w in range(terms):
            l2[q, row[w] : row[w] + n, :] = wide(lf[w, q] * mask[w, q].astype(F32))
    loads[1].wait()
    for q in range(blocks):
        for d in (-1, 0, 1):
            if 0 <= q + d < blocks:
                for w in groups[d]:
                    r2[q, row[w] : row[w] + n, :] = wide(rt[w, q + d])
    loads[2].wait()

    @pl.when(seg == 0)
    def _():
        here = lax.broadcasted_iota(jnp.int32, (n, n), 0)
        across = lax.broadcasted_iota(jnp.int32, (n, n), 1)
        for q in range(blocks):
            amat[q] = (here == across).astype(F32)

    for j in range(n_seg - 1):
        @pl.when(j < seg)
        def _():
            m_arrival(j).wait_recv()
            for q in range(blocks):
                if j == 0:
                    amat[q] = mp[0, q]
                else:
                    amat[q] = halves(dot(wide(amat[q]), twice(mp[j, q])))

    for q in range(blocks):
        a = amat[q]
        turned = wide(a.T)
        doubled = twice(a)
        for d in (-1, 0, 1):
            for w in groups[d]:
                part = halves(dot(l2[q, row[w] : row[w] + n, :], doubled))
                l2[q, row[w] : row[w] + n, :] = wide(halves(dot(turned, twice(part))))

    def contribution(q, d, vector2):
        size = len(groups[d]) * n
        x = halves(dot(l2[q, start[d] : start[d] + size, :], vector2))
        x = jnp.concatenate([x[i * n : (i + 1) * n] for i in range(len(groups[d]))], axis=1)
        x = jnp.concatenate(split(x), axis=0)
        y = halves(dot(x, r2[q, start[d] : start[d] + size, :]))
        return y[:n] + y[n:]

    def step(t, _):
        own = [twice(vs[t, q]) for q in range(blocks)]
        image = []
        for q in range(blocks):
            total = None
            for d in (-1, 0, 1):
                if 0 <= q + d < blocks:
                    y = contribution(q, d, own[q + d])
                    total = y if total is None else total + y
            vs[t + 1, q] = total

        tile = jnp.zeros((8, n), F32)
        for side, there in ((0, has_low), (1, has_high)):
            q, d = (0, -1) if side == 0 else (blocks - 1, 1)

            @pl.when(there & (t == 0))
            def _():
                for copy in r_arrivals(side):
                    copy.wait_recv()

            @pl.when(t == 0)
            def _():
                for i, w in enumerate(groups[d]):
                    r2[q, row[w] : row[w] + n, :] = wide(rhalo[side, i])

            @pl.when(there)
            def _():
                v_arrival(t, side).wait_recv()

            vs[t + 1, q] = vs[t + 1, q] + contribution(q, d, twice(vh[t, side]))
            if blocks > 1:
                @pl.when(there & (t < ITERS - 1))
                def _():
                    v_copy(t + 1, vs.at[t + 1, q], side).start()

        if blocks == 1:
            for side, there in ((0, has_low), (1, has_high)):
                @pl.when(there & (t < ITERS - 1))
                def _():
                    v_copy(t + 1, vs.at[t + 1, 0], side).start()

        @pl.when(t < ITERS - 1)
        def _():
            total = squares(vs[t + 1, 0])
            for q in range(1, blocks):
                total = total + squares(vs[t + 1, q])
            red[t // 2, sec, t % 2] = total

        @pl.when(t == 1)
        def _():
            for d in range(1, n_sec):
                s_copy(0, d).start()

        return 0

    lax.fori_loop(0, ITERS, step, 0)

    cells = n_sec * blocks * n * n

    def whole(stage):
        total = red[stage, 0]
        for other in range(1, n_sec):
            total = total + red[stage, other]
        first = jnp.sum(total[0], keepdims=True)
        second = jnp.sum(total[1], keepdims=True)
        return first / cells, second / cells

    for d in range(1, n_sec):
        s_arrival(0, d).wait_recv()
    m1, m2 = whole(0)
    s1 = lax.rsqrt(m1 + EPS)
    s12 = s1 * lax.rsqrt(s1 * s1 * m2 + EPS)
    last = [vs[ITERS, q] * s12 for q in range(blocks)]
    total = squares(last[0])
    for q in range(1, blocks):
        total = total + squares(last[q])
    red[1, sec, 1] = total
    for d in range(1, n_sec):
        s_copy(1, d).start()

    here = lax.broadcasted_iota(jnp.int32, (n, n), 0)
    across = lax.broadcasted_iota(jnp.int32, (n, n), 1)
    for q in range(blocks):
        theta_out[0, q] = last[q]
        kept = ((here < ranks[0, q]) & (across < ranks[0, q])).astype(F32)
        density[0, q] = halves(dot(wide(last[q]), twice(last[q].T))) * kept

    for d in range(1, n_sec):
        s_arrival(1, d).wait_recv()
    m3, m4 = whole(1)
    s3 = lax.rsqrt(s12 * s12 * m3 + EPS)
    s34 = s3 * lax.rsqrt(s3 * s3 * m4 + EPS)
    for q in range(blocks):
        theta_out[0, q] = theta_out[0, q] * s34
        density[0, q] = density[0, q] * (s34 * s34 / n)

    for d in range(1, n_seg):
        @pl.when(seg + d < n_seg)
        def _():
            m_copy(d).wait_send()
    for side, there in ((0, has_low), (1, has_high)):
        q = 0 if side == 0 else blocks - 1
        @pl.when(there)
        def _():
            v_copy(0, theta.at[0, q], side).wait_send()
            for t in range(1, ITERS):
                v_copy(t, vs.at[t, q], side).wait_send()
            for copy in r_copies(side):
                copy.wait_send()
    for stage in range(2):
        for d in range(1, n_sec):
            s_copy(stage, d).wait_send()


def per_device(n_seg, n_sec, theta_in, left_env, site_maps, right_env, mpo_mask, ranks):
    terms, blocks, n, _ = left_env.shape
    groups = {d: [w for w in range(terms) if w % 3 - 1 == d] for d in (-1, 0, 1)}
    most = max(len(g) for g in groups.values())
    block = (n, n)
    anywhere = pl.BlockSpec(memory_space=pl.ANY)
    scalars = pl.BlockSpec(memory_space=pltpu.SMEM)
    vmem = pl.BlockSpec(memory_space=pltpu.VMEM)
    out = jax.ShapeDtypeStruct(theta_in.shape, F32)
    dma = pltpu.SemaphoreType.DMA
    return pl.pallas_call(
        functools.partial(kernel, n_seg, n_sec, groups),
        out_shape=(out, out),
        in_specs=[anywhere, anywhere, anywhere, anywhere, scalars, scalars],
        out_specs=(vmem, vmem),
        scratch_shapes=[
            pltpu.VMEM((terms, blocks) + block, F32),
            pltpu.VMEM((terms, blocks) + block, F32),
            pltpu.VMEM((n_seg, blocks) + block, F32),
            pltpu.VMEM((blocks,) + block, F32),
            pltpu.VMEM((2, most) + block, F32),
            pltpu.VMEM((ITERS, 2) + block, F32),
            pltpu.VMEM((ITERS + 1, blocks) + block, F32),
            pltpu.VMEM((blocks, terms * n, 2 * n), BF16),
            pltpu.VMEM((blocks, terms * n, 2 * n), BF16),
            pltpu.VMEM((2, n_sec, 2, 8, n), F32),
            dma((3,)),
            dma((n_seg,)),
            dma((n_seg,)),
            dma((2, most)),
            dma((2, most)),
            dma((ITERS, 2)),
            dma((ITERS, 2)),
            dma((2, n_sec)),
            dma((2, n_sec)),
        ],
        compiler_params=pltpu.CompilerParams(
            collective_id=0, has_side_effects=True, vmem_limit_bytes=48 * 1024 * 1024
        ),
        cost_estimate=pl.CostEstimate(flops=2 * n**3 * 4 * 200, bytes_accessed=4 * n * n * 60, transcendentals=0),
    )(theta_in, left_env, site_maps, right_env, mpo_mask, ranks)


def solution(mesh):
    n_seg, n_sec = mesh.shape["seg"], mesh.shape["sec"]
    return jax.shard_map(
        functools.partial(per_device, n_seg, n_sec),
        mesh=mesh,
        in_specs=(
            P("seg", "sec", None, None),
            P(None, "sec", None, None),
            P("seg", "sec", None, None),
            P("seg", None, "sec", None, None),
            P(None, "sec"),
            P("seg", "sec"),
        ),
        out_specs=(P("seg", "sec", None, None), P("seg", "sec", None, None)),
        check_vma=False,
    )
```

```python
import functools

import jax
import jax.numpy as jnp
from jax import lax
from jax.experimental import pallas as pl
from jax.experimental.pallas import tpu as pltpu
from jax.sharding import PartitionSpec as P

ITERS = 4
EPS = 1e-06
MESH = pl.DeviceIdType.MESH
F32, BF16 = jnp.float32, jnp.bfloat16


def split(x):
    high = x.astype(BF16)
    low = (x - high.astype(F32)).astype(BF16)
    return high, low


def wide(x):
    return jnp.concatenate(split(x), axis=1)


def twice(x):
    pair = wide(x)
    return jnp.concatenate([pair, pair], axis=0)


def dot(a, b):
    return lax.dot_general(a, b, (((1,), (0,)), ((), ())), preferred_element_type=F32)


def halves(x):
    n = x.shape[1] // 2
    return x[:, :n] + x[:, n:]


def squares(x):
    return jnp.sum((x * x).reshape(-1, 8, x.shape[1]), axis=0)


def kernel(
    n_seg, n_sec, groups, theta, left, maps, right, mask, ranks, theta_out, density,
    lf, rt, mp, amat, rhalo, vh, vs, l2, r2, red,
    local_sem, m_send, m_recv, r_send, r_recv, v_send, v_recv, s_send, s_recv,
):
    seg, sec = lax.axis_index("seg"), lax.axis_index("sec")
    blocks, n = theta.shape[1], theta.shape[2]
    terms = left.shape[0]
    has_low, has_high = sec > 0, sec < n_sec - 1
    row = {}
    start = {}
    for d in (-1, 0, 1):
        start[d] = len(row) * n
        for w in groups[d]:
            row[w] = len(row) * n

    loads = [
        pltpu.make_async_copy(left, lf, local_sem.at[0]),
        pltpu.make_async_copy(right.at[0], rt, local_sem.at[1]),
        pltpu.make_async_copy(theta.at[0], vs.at[0], local_sem.at[2]),
    ]
    for load in loads:
        load.start()

    barrier = pltpu.get_barrier_semaphore()
    for d in range(1, n_seg):
        pl.semaphore_signal(barrier, inc=1, device_id={"seg": lax.rem(seg + d, n_seg)}, device_id_type=MESH)
    for d in range(1, n_sec):
        pl.semaphore_signal(barrier, inc=1, device_id={"sec": lax.rem(sec + d, n_sec)}, device_id_type=MESH)
    pl.semaphore_wait(barrier, n_seg + n_sec - 2)

    def m_copy(d):
        return pltpu.make_async_remote_copy(
            src_ref=maps.at[0], dst_ref=mp.at[seg], send_sem=m_send.at[d - 1], recv_sem=m_recv.at[seg],
            device_id={"seg": seg + d}, device_id_type=MESH,
        )

    def m_arrival(j):
        return pltpu.make_async_remote_copy(
            src_ref=maps.at[0], dst_ref=mp.at[j], send_sem=m_send.at[0], recv_sem=m_recv.at[j],
            device_id={"seg": j}, device_id_type=MESH,
        )

    def v_copy(t, source, side):
        other = sec - 1 if side == 0 else sec + 1
        return pltpu.make_async_remote_copy(
            src_ref=source, dst_ref=vh.at[t, 1 - side], send_sem=v_send.at[t, side],
            recv_sem=v_recv.at[t, 1 - side], device_id={"sec": other}, device_id_type=MESH,
        )

    def v_arrival(t, side):
        other = sec - 1 if side == 0 else sec + 1
        return pltpu.make_async_remote_copy(
            src_ref=vs.at[0, 0], dst_ref=vh.at[t, side], send_sem=v_send.at[t, side],
            recv_sem=v_recv.at[t, side], device_id={"sec": other}, device_id_type=MESH,
        )

    def r_copies(side):
        other = sec - 1 if side == 0 else sec + 1
        q, shift = (0, 1) if side == 0 else (blocks - 1, -1)
        return [
            pltpu.make_async_remote_copy(
                src_ref=right.at[0, w, q], dst_ref=rhalo.at[1 - side, i], send_sem=r_send.at[side, i],
                recv_sem=r_recv.at[1 - side, i], device_id={"sec": other}, device_id_type=MESH,
            )
            for i, w in enumerate(groups[shift])
        ]

    def r_arrivals(side):
        other = sec - 1 if side == 0 else sec + 1
        shift = -1 if side == 0 else 1
        return [
            pltpu.make_async_remote_copy(
                src_ref=right.at[0, w, 0], dst_ref=rhalo.at[side, i], send_sem=r_send.at[side, i],
                recv_sem=r_recv.at[side, i], device_id={"sec": other}, device_id_type=MESH,
            )
            for i, w in enumerate(groups[shift])
        ]

    def s_copy(stage, d):
        return pltpu.make_async_remote_copy(
            src_ref=red.at[stage, sec], dst_ref=red.at[stage, sec], send_sem=s_send.at[stage, d],
            recv_sem=s_recv.at[stage, sec], device_id={"sec": lax.rem(sec + d, n_sec)}, device_id_type=MESH,
        )

    def s_arrival(stage, d):
        other = lax.rem(sec + d, n_sec)
        return pltpu.make_async_remote_copy(
            src_ref=red.at[stage, sec], dst_ref=red.at[stage, other], send_sem=s_send.at[stage, d],
            recv_sem=s_recv.at[stage, other], device_id={"sec": other}, device_id_type=MESH,
        )

    for d in range(1, n_seg):
        @pl.when(seg + d < n_seg)
        def _():
            m_copy(d).start()

    for side, there in ((0, has_low), (1, has_high)):
        q = 0 if side == 0 else blocks - 1
        @pl.when(there)
        def _():
            v_copy(0, theta.at[0, q], side).start()
            for copy in r_copies(side):
                copy.start()

        @pl.when(jnp.logical_not(there))
        def _():
            rhalo[side] = jnp.zeros_like(rhalo[side])
            for t in range(ITERS):
                vh[t, side] = jnp.zeros_like(vh[t, side])

    loads[0].wait()
    for q in range(blocks):
        for w in range(terms):
            l2[q, row[w] : row[w] + n, :] = wide(lf[w, q] * mask[q, w].astype(F32))
    loads[1].wait()
    for q in range(blocks):
        for d in (-1, 0, 1):
            if 0 <= q + d < blocks:
                for w in groups[d]:
                    r2[q, row[w] : row[w] + n, :] = wide(rt[w, q + d])
    loads[2].wait()

    @pl.when(seg == 0)
    def _():
        here = lax.broadcasted_iota(jnp.int32, (n, n), 0)
        across = lax.broadcasted_iota(jnp.int32, (n, n), 1)
        for q in range(blocks):
            amat[q] = (here == across).astype(F32)

    for j in range(n_seg - 1):
        @pl.when(j < seg)
        def _():
            m_arrival(j).wait_recv()
            for q in range(blocks):
                if j == 0:
                    amat[q] = mp[0, q]
                else:
                    amat[q] = halves(dot(wide(amat[q]), twice(mp[j, q])))

    for q in range(blocks):
        a = amat[q]
        turned = wide(a.T)
        doubled = twice(a)
        for d in (-1, 0, 1):
            for w in groups[d]:
                part = halves(dot(l2[q, row[w] : row[w] + n, :], doubled))
                l2[q, row[w] : row[w] + n, :] = wide(halves(dot(turned, twice(part))))

    def contribution(q, d, vector2):
        size = len(groups[d]) * n
        x = halves(dot(l2[q, start[d] : start[d] + size, :], vector2))
        x = jnp.concatenate([x[i * n : (i + 1) * n] for i in range(len(groups[d]))], axis=1)
        x = jnp.concatenate(split(x), axis=0)
        y = halves(dot(x, r2[q, start[d] : start[d] + size, :]))
        return y[:n] + y[n:]

    def step(t, _):
        own = [twice(vs[t, q]) for q in range(blocks)]
        image = []
        for q in range(blocks):
            total = None
            for d in (-1, 0, 1):
                if 0 <= q + d < blocks:
                    y = contribution(q, d, own[q + d])
                    total = y if total is None else total + y
            vs[t + 1, q] = total

        sides = ((0, has_low, 0, -1), (1, has_high, blocks - 1, 1))

        @pl.when(t == 0)
        def _():
            for side, there, q, d in sides:
                @pl.when(there)
                def _():
                    for copy in r_arrivals(side):
                        copy.wait_recv()

            for side, there, q, d in sides:
                for i, w in enumerate(groups[d]):
                    r2[q, row[w] : row[w] + n, :] = wide(rhalo[side, i])

        for side, there, q, d in sides:
            @pl.when(there)
            def _():
                v_arrival(t, side).wait_recv()

        crossed = [contribution(q, d, twice(vh[t, side])) for side, _, q, d in sides]
        for side, there, q, d in sides:
            vs[t + 1, q] = vs[t + 1, q] + crossed[side]
        for side, there, q, d in sides:
            @pl.when(there & (t < ITERS - 1))
            def _():
                v_copy(t + 1, vs.at[t + 1, q], side).start()

        @pl.when(t < ITERS - 1)
        def _():
            total = squares(vs[t + 1, 0])
            for q in range(1, blocks):
                total = total + squares(vs[t + 1, q])
            red[t // 2, sec, t % 2] = total

        @pl.when(t == 1)
        def _():
            for d in range(1, n_sec):
                s_copy(0, d).start()

        return 0

    lax.fori_loop(0, ITERS, step, 0)

    cells = n_sec * blocks * n * n

    def whole(stage):
        total = red[stage, 0]
        for other in range(1, n_sec):
            total = total + red[stage, other]
        first = jnp.sum(total[0], keepdims=True)
        second = jnp.sum(total[1], keepdims=True)
        return first / cells, second / cells

    for d in range(1, n_sec):
        s_arrival(0, d).wait_recv()
    m1, m2 = whole(0)
    s1 = lax.rsqrt(m1 + EPS)
    s12 = s1 * lax.rsqrt(s1 * s1 * m2 + EPS)
    last = [vs[ITERS, q] * s12 for q in range(blocks)]
    total = squares(last[0])
    for q in range(1, blocks):
        total = total + squares(last[q])
    red[1, sec, 1] = total
    for d in range(1, n_sec):
        s_copy(1, d).start()

    here = lax.broadcasted_iota(jnp.int32, (n, n), 0)
    across = lax.broadcasted_iota(jnp.int32, (n, n), 1)
    for q in range(blocks):
        theta_out[0, q] = last[q]
        kept = ((here < ranks[0, q]) & (across < ranks[0, q])).astype(F32)
        density[0, q] = halves(dot(wide(last[q]), twice(last[q].T))) * kept

    for d in range(1, n_sec):
        s_arrival(1, d).wait_recv()
    m3, m4 = whole(1)
    s3 = lax.rsqrt(s12 * s12 * m3 + EPS)
    s34 = s3 * lax.rsqrt(s3 * s3 * m4 + EPS)
    for q in range(blocks):
        theta_out[0, q] = theta_out[0, q] * s34
        density[0, q] = density[0, q] * (s34 * s34 / n)

    for d in range(1, n_seg):
        @pl.when(seg + d < n_seg)
        def _():
            m_copy(d).wait_send()
    for side, there in ((0, has_low), (1, has_high)):
        q = 0 if side == 0 else blocks - 1
        @pl.when(there)
        def _():
            v_copy(0, theta.at[0, q], side).wait_send()
            for t in range(1, ITERS):
                v_copy(t, vs.at[t, q], side).wait_send()
            for copy in r_copies(side):
                copy.wait_send()
    for stage in range(2):
        for d in range(1, n_sec):
            s_copy(stage, d).wait_send()


def per_device(n_seg, n_sec, theta_in, left_env, site_maps, right_env, mpo_mask, ranks):
    terms, blocks, n, _ = left_env.shape
    groups = {d: [w for w in range(terms) if w % 3 - 1 == d] for d in (-1, 0, 1)}
    most = max(len(g) for g in groups.values())
    block = (n, n)
    anywhere = pl.BlockSpec(memory_space=pl.ANY)
    scalars = pl.BlockSpec(memory_space=pltpu.SMEM)
    vmem = pl.BlockSpec(memory_space=pltpu.VMEM)
    out = jax.ShapeDtypeStruct(theta_in.shape, F32)
    dma = pltpu.SemaphoreType.DMA
    return pl.pallas_call(
        functools.partial(kernel, n_seg, n_sec, groups),
        out_shape=(out, out),
        in_specs=[anywhere, anywhere, anywhere, anywhere, scalars, scalars],
        out_specs=(vmem, vmem),
        scratch_shapes=[
            pltpu.VMEM((terms, blocks) + block, F32),
            pltpu.VMEM((terms, blocks) + block, F32),
            pltpu.VMEM((n_seg, blocks) + block, F32),
            pltpu.VMEM((blocks,) + block, F32),
            pltpu.VMEM((2, most) + block, F32),
            pltpu.VMEM((ITERS, 2) + block, F32),
            pltpu.VMEM((ITERS + 1, blocks) + block, F32),
            pltpu.VMEM((blocks, terms * n, 2 * n), BF16),
            pltpu.VMEM((blocks, terms * n, 2 * n), BF16),
            pltpu.VMEM((2, n_sec, 2, 8, n), F32),
            dma((3,)),
            dma((n_seg,)),
            dma((n_seg,)),
            dma((2, most)),
            dma((2, most)),
            dma((ITERS, 2)),
            dma((ITERS, 2)),
            dma((2, n_sec)),
            dma((2, n_sec)),
        ],
        compiler_params=pltpu.CompilerParams(
            collective_id=0, has_side_effects=True
        ),
        cost_estimate=pl.CostEstimate(flops=2 * n**3 * 4 * 200, bytes_accessed=4 * n * n * 60, transcendentals=0),
    )(theta_in, left_env, site_maps, right_env, mpo_mask.T, ranks)


def solution(mesh):
    n_seg, n_sec = mesh.shape["seg"], mesh.shape["sec"]
    return jax.shard_map(
        functools.partial(per_device, n_seg, n_sec),
        mesh=mesh,
        in_specs=(
            P("seg", "sec", None, None),
            P(None, "sec", None, None),
            P("seg", "sec", None, None),
            P("seg", None, "sec", None, None),
            P(None, "sec"),
            P("seg", "sec"),
        ),
        out_specs=(P("seg", "sec", None, None), P("seg", "sec", None, None)),
        check_vma=False,
    )
```

```python
import functools

import jax
import jax.numpy as jnp
from jax import lax
from jax.experimental import pallas as pl
from jax.experimental.pallas import tpu as pltpu
from jax.sharding import PartitionSpec as P

ITERS = 4
EPS = 1e-06
MESH = pl.DeviceIdType.MESH
F32, BF16 = jnp.float32, jnp.bfloat16


def split(x):
    high = x.astype(BF16)
    low = (x - high.astype(F32)).astype(BF16)
    return high, low


def wide(x):
    return jnp.concatenate(split(x), axis=1)


def twice(x):
    pair = wide(x)
    return jnp.concatenate([pair, pair], axis=0)


def dot(a, b):
    return lax.dot_general(a, b, (((1,), (0,)), ((), ())), preferred_element_type=F32)


def halves(x):
    n = x.shape[1] // 2
    return x[:, :n] + x[:, n:]


def squares(x):
    return jnp.sum((x * x).reshape(-1, 8, x.shape[1]), axis=0)


def kernel(
    n_seg, n_sec, groups, theta, left, maps, right, mask, ranks, theta_out, density,
    lf, rt, mp, amat, rhalo, vh, vs, l2, r2, red,
    local_sem, m_send, m_recv, m_pass, r_send, r_recv, v_send, v_recv, s_send, s_recv,
):
    seg, sec = lax.axis_index("seg"), lax.axis_index("sec")
    blocks, n = theta.shape[1], theta.shape[2]
    terms = left.shape[0]
    has_low, has_high = sec > 0, sec < n_sec - 1
    row = {}
    start = {}
    for d in (-1, 0, 1):
        start[d] = len(row) * n
        for w in groups[d]:
            row[w] = len(row) * n

    loads = [
        pltpu.make_async_copy(left, lf, local_sem.at[0]),
        pltpu.make_async_copy(right.at[0], rt, local_sem.at[1]),
        pltpu.make_async_copy(theta.at[0], vs.at[0], local_sem.at[2]),
    ]
    for load in loads:
        load.start()

    barrier = pltpu.get_barrier_semaphore()
    for d in range(1, n_seg):
        pl.semaphore_signal(barrier, inc=1, device_id={"seg": lax.rem(seg + d, n_seg)}, device_id_type=MESH)
    for d in range(1, n_sec):
        pl.semaphore_signal(barrier, inc=1, device_id={"sec": lax.rem(sec + d, n_sec)}, device_id_type=MESH)
    pl.semaphore_wait(barrier, n_seg + n_sec - 2)

    def m_copy(d):
        return pltpu.make_async_remote_copy(
            src_ref=maps.at[0], dst_ref=mp.at[seg], send_sem=m_send.at[d - 1], recv_sem=m_recv.at[seg],
            device_id={"seg": seg + d}, device_id_type=MESH,
        )

    def m_arrival(j):
        return pltpu.make_async_remote_copy(
            src_ref=maps.at[0], dst_ref=mp.at[j], send_sem=m_send.at[0], recv_sem=m_recv.at[j],
            device_id={"seg": j}, device_id_type=MESH,
        )

    def m_relay(j):
        other = seg + 1 - 2 * lax.rem(seg, 2)
        return pltpu.make_async_remote_copy(
            src_ref=mp.at[j], dst_ref=mp.at[j], send_sem=m_pass.at[j], recv_sem=m_recv.at[j],
            device_id={"seg": other}, device_id_type=MESH,
        )

    def m_direct(j):
        return (j < seg) & (lax.rem(seg + j, 2) == 0)

    def v_copy(t, source, side):
        other = sec - 1 if side == 0 else sec + 1
        return pltpu.make_async_remote_copy(
            src_ref=source, dst_ref=vh.at[t, 1 - side], send_sem=v_send.at[t, side],
            recv_sem=v_recv.at[t, 1 - side], device_id={"sec": other}, device_id_type=MESH,
        )

    def v_arrival(t, side):
        other = sec - 1 if side == 0 else sec + 1
        return pltpu.make_async_remote_copy(
            src_ref=vs.at[0, 0], dst_ref=vh.at[t, side], send_sem=v_send.at[t, side],
            recv_sem=v_recv.at[t, side], device_id={"sec": other}, device_id_type=MESH,
        )

    def r_copies(side):
        other = sec - 1 if side == 0 else sec + 1
        q, shift = (0, 1) if side == 0 else (blocks - 1, -1)
        return [
            pltpu.make_async_remote_copy(
                src_ref=right.at[0, w, q], dst_ref=rhalo.at[1 - side, i], send_sem=r_send.at[side, i],
                recv_sem=r_recv.at[1 - side, i], device_id={"sec": other}, device_id_type=MESH,
            )
            for i, w in enumerate(groups[shift])
        ]

    def r_arrivals(side):
        other = sec - 1 if side == 0 else sec + 1
        shift = -1 if side == 0 else 1
        return [
            pltpu.make_async_remote_copy(
                src_ref=right.at[0, w, 0], dst_ref=rhalo.at[side, i], send_sem=r_send.at[side, i],
                recv_sem=r_recv.at[side, i], device_id={"sec": other}, device_id_type=MESH,
            )
            for i, w in enumerate(groups[shift])
        ]

    def s_copy(stage, d):
        return pltpu.make_async_remote_copy(
            src_ref=red.at[stage, sec], dst_ref=red.at[stage, sec], send_sem=s_send.at[stage, d],
            recv_sem=s_recv.at[stage, sec], device_id={"sec": lax.rem(sec + d, n_sec)}, device_id_type=MESH,
        )

    def s_arrival(stage, d):
        other = lax.rem(sec + d, n_sec)
        return pltpu.make_async_remote_copy(
            src_ref=red.at[stage, sec], dst_ref=red.at[stage, other], send_sem=s_send.at[stage, d],
            recv_sem=s_recv.at[stage, other], device_id={"sec": other}, device_id_type=MESH,
        )

    def m_goes(d):
        return lax.rem(seg, 2) == 0 if d == 1 else seg + d < n_seg

    m_ways = [1] + list(range(2, n_seg, 2))
    for d in reversed(m_ways):
        @pl.when(m_goes(d))
        def _():
            m_copy(d).start()

    for side, there in ((0, has_low), (1, has_high)):
        q = 0 if side == 0 else blocks - 1
        @pl.when(there)
        def _():
            v_copy(0, theta.at[0, q], side).start()
            for copy in r_copies(side):
                copy.start()

        @pl.when(jnp.logical_not(there))
        def _():
            rhalo[side] = jnp.zeros_like(rhalo[side])
            for t in range(ITERS):
                vh[t, side] = jnp.zeros_like(vh[t, side])

    loads[0].wait()
    for q in range(blocks):
        for w in range(terms):
            l2[q, row[w] : row[w] + n, :] = wide(lf[w, q] * mask[q, w].astype(F32))
    loads[1].wait()
    for q in range(blocks):
        for d in (-1, 0, 1):
            if 0 <= q + d < blocks:
                for w in groups[d]:
                    r2[q, row[w] : row[w] + n, :] = wide(rt[w, q + d])
    loads[2].wait()

    for j in range(n_seg - 2):
        @pl.when(m_direct(j))
        def _():
            m_arrival(j).wait_recv()
            m_relay(j).start()

    @pl.when(seg == 0)
    def _():
        here = lax.broadcasted_iota(jnp.int32, (n, n), 0)
        across = lax.broadcasted_iota(jnp.int32, (n, n), 1)
        for q in range(blocks):
            amat[q] = (here == across).astype(F32)

    for j in range(n_seg - 1):
        @pl.when((j < seg) & jnp.logical_not(m_direct(j)))
        def _():
            m_arrival(j).wait_recv()

        @pl.when(j < seg)
        def _():
            for q in range(blocks):
                if j == 0:
                    amat[q] = mp[0, q]
                else:
                    amat[q] = halves(dot(wide(amat[q]), twice(mp[j, q])))

    for q in range(blocks):
        a = amat[q]
        turned = wide(a.T)
        doubled = twice(a)
        for d in (-1, 0, 1):
            for w in groups[d]:
                part = halves(dot(l2[q, row[w] : row[w] + n, :], doubled))
                l2[q, row[w] : row[w] + n, :] = wide(halves(dot(turned, twice(part))))

    def contribution(q, d, vector2):
        size = len(groups[d]) * n
        x = halves(dot(l2[q, start[d] : start[d] + size, :], vector2))
        x = jnp.concatenate([x[i * n : (i + 1) * n] for i in range(len(groups[d]))], axis=1)
        x = jnp.concatenate(split(x), axis=0)
        y = halves(dot(x, r2[q, start[d] : start[d] + size, :]))
        return y[:n] + y[n:]

    def step(t, _):
        own = [twice(vs[t, q]) for q in range(blocks)]
        image = []
        for q in range(blocks):
            total = None
            for d in (-1, 0, 1):
                if 0 <= q + d < blocks:
                    y = contribution(q, d, own[q + d])
                    total = y if total is None else total + y
            vs[t + 1, q] = total

        sides = ((0, has_low, 0, -1), (1, has_high, blocks - 1, 1))

        @pl.when(t == 0)
        def _():
            for side, there, q, d in sides:
                @pl.when(there)
                def _():
                    for copy in r_arrivals(side):
                        copy.wait_recv()

            for side, there, q, d in sides:
                for i, w in enumerate(groups[d]):
                    r2[q, row[w] : row[w] + n, :] = wide(rhalo[side, i])

        for side, there, q, d in sides:
            @pl.when(there)
            def _():
                v_arrival(t, side).wait_recv()

        crossed = [contribution(q, d, twice(vh[t, side])) for side, _, q, d in sides]
        for side, there, q, d in sides:
            vs[t + 1, q] = vs[t + 1, q] + crossed[side]
        for side, there, q, d in sides:
            @pl.when(there & (t < ITERS - 1))
            def _():
                v_copy(t + 1, vs.at[t + 1, q], side).start()

        @pl.when(t < ITERS - 1)
        def _():
            total = squares(vs[t + 1, 0])
            for q in range(1, blocks):
                total = total + squares(vs[t + 1, q])
            red[t // 2, sec, t % 2] = total

        @pl.when(t == 1)
        def _():
            for d in range(1, n_sec):
                s_copy(0, d).start()

        return 0

    lax.fori_loop(0, ITERS, step, 0)

    cells = n_sec * blocks * n * n

    def whole(stage):
        total = red[stage, 0]
        for other in range(1, n_sec):
            total = total + red[stage, other]
        first = jnp.sum(total[0], keepdims=True)
        second = jnp.sum(total[1], keepdims=True)
        return first / cells, second / cells

    for d in range(1, n_sec):
        s_arrival(0, d).wait_recv()
    m1, m2 = whole(0)
    s1 = lax.rsqrt(m1 + EPS)
    s12 = s1 * lax.rsqrt(s1 * s1 * m2 + EPS)
    last = [vs[ITERS, q] * s12 for q in range(blocks)]
    total = squares(last[0])
    for q in range(1, blocks):
        total = total + squares(last[q])
    red[1, sec, 1] = total
    for d in range(1, n_sec):
        s_copy(1, d).start()

    here = lax.broadcasted_iota(jnp.int32, (n, n), 0)
    across = lax.broadcasted_iota(jnp.int32, (n, n), 1)
    for q in range(blocks):
        theta_out[0, q] = last[q]
        kept = ((here < ranks[0, q]) & (across < ranks[0, q])).astype(F32)
        density[0, q] = halves(dot(wide(last[q]), twice(last[q].T))) * kept

    for d in range(1, n_sec):
        s_arrival(1, d).wait_recv()
    m3, m4 = whole(1)
    s3 = lax.rsqrt(s12 * s12 * m3 + EPS)
    s34 = s3 * lax.rsqrt(s3 * s3 * m4 + EPS)
    for q in range(blocks):
        theta_out[0, q] = theta_out[0, q] * s34
        density[0, q] = density[0, q] * (s34 * s34 / n)

    for d in m_ways:
        @pl.when(m_goes(d))
        def _():
            m_copy(d).wait_send()
    for j in range(n_seg - 2):
        @pl.when(m_direct(j))
        def _():
            m_relay(j).wait_send()
    for side, there in ((0, has_low), (1, has_high)):
        q = 0 if side == 0 else blocks - 1
        @pl.when(there)
        def _():
            v_copy(0, theta.at[0, q], side).wait_send()
            for t in range(1, ITERS):
                v_copy(t, vs.at[t, q], side).wait_send()
            for copy in r_copies(side):
                copy.wait_send()
    for stage in range(2):
        for d in range(1, n_sec):
            s_copy(stage, d).wait_send()


def per_device(n_seg, n_sec, theta_in, left_env, site_maps, right_env, mpo_mask, ranks):
    terms, blocks, n, _ = left_env.shape
    groups = {d: [w for w in range(terms) if w % 3 - 1 == d] for d in (-1, 0, 1)}
    most = max(len(g) for g in groups.values())
    block = (n, n)
    anywhere = pl.BlockSpec(memory_space=pltpu.HBM)
    scalars = pl.BlockSpec(memory_space=pltpu.SMEM)
    vmem = pl.BlockSpec(memory_space=pltpu.VMEM)
    out = jax.ShapeDtypeStruct(theta_in.shape, F32)
    dma = pltpu.SemaphoreType.DMA
    return pl.pallas_call(
        functools.partial(kernel, n_seg, n_sec, groups),
        out_shape=(out, out),
        in_specs=[anywhere, anywhere, anywhere, anywhere, scalars, scalars],
        out_specs=(vmem, vmem),
        scratch_shapes=[
            pltpu.VMEM((terms, blocks) + block, F32),
            pltpu.VMEM((terms, blocks) + block, F32),
            pltpu.VMEM((n_seg, blocks) + block, F32),
            pltpu.VMEM((blocks,) + block, F32),
            pltpu.VMEM((2, most) + block, F32),
            pltpu.VMEM((ITERS, 2) + block, F32),
            pltpu.VMEM((ITERS + 1, blocks) + block, F32),
            pltpu.VMEM((blocks, terms * n, 2 * n), BF16),
            pltpu.VMEM((blocks, terms * n, 2 * n), BF16),
            pltpu.VMEM((2, n_sec, 2, 8, n), F32),
            dma((3,)),
            dma((n_seg,)),
            dma((n_seg,)),
            dma((n_seg,)),
            dma((2, most)),
            dma((2, most)),
            dma((ITERS, 2)),
            dma((ITERS, 2)),
            dma((2, n_sec)),
            dma((2, n_sec)),
        ],
        compiler_params=pltpu.CompilerParams(
            collective_id=0, has_side_effects=True, vmem_limit_bytes=40 * 1024 * 1024
        ),
        cost_estimate=pl.CostEstimate(flops=2 * n**3 * 4 * 200, bytes_accessed=4 * n * n * 60, transcendentals=0),
    )(theta_in, left_env, site_maps, right_env, mpo_mask.T, ranks)


def solution(mesh):
    n_seg, n_sec = mesh.shape["seg"], mesh.shape["sec"]
    return jax.shard_map(
        functools.partial(per_device, n_seg, n_sec),
        mesh=mesh,
        in_specs=(
            P("seg", "sec", None, None),
            P(None, "sec", None, None),
            P("seg", "sec", None, None),
            P("seg", None, "sec", None, None),
            P(None, "sec"),
            P("seg", "sec"),
        ),
        out_specs=(P("seg", "sec", None, None), P("seg", "sec", None, None)),
        check_vma=False,
    )
```

```python
import functools

import jax
import jax.numpy as jnp
from jax import lax
from jax.experimental import pallas as pl
from jax.experimental.pallas import tpu as pltpu
from jax.sharding import PartitionSpec as P

ITERS = 4
EPS = 1e-06
MESH = pl.DeviceIdType.MESH
F32, BF16 = jnp.float32, jnp.bfloat16


def split(x):
    high = x.astype(BF16)
    low = (x - high.astype(F32)).astype(BF16)
    return high, low


def wide(x):
    return jnp.concatenate(split(x), axis=1)


def twice(x):
    pair = wide(x)
    return jnp.concatenate([pair, pair], axis=0)


def dot(a, b):
    return lax.dot_general(a, b, (((1,), (0,)), ((), ())), preferred_element_type=F32)


def halves(x):
    n = x.shape[1] // 2
    return x[:, :n] + x[:, n:]


def squares(x):
    return jnp.sum((x * x).reshape(-1, 8, x.shape[1]), axis=0)


def kernel(
    n_seg, n_sec, groups, theta, left, maps, right, mask, ranks, theta_out, density,
    lf, rt, mp, amat, rhalo, vh, vs, l2, r2, red,
    local_sem, m_send, m_recv, m_pass, r_send, r_recv, v_send, v_recv, s_send, s_recv,
):
    seg, sec = lax.axis_index("seg"), lax.axis_index("sec")
    blocks, n = theta.shape[1], theta.shape[2]
    terms = left.shape[0]
    has_low, has_high = sec > 0, sec < n_sec - 1
    row = {}
    start = {}
    for d in (-1, 0, 1):
        start[d] = len(row) * n
        for w in groups[d]:
            row[w] = len(row) * n

    loads = [
        pltpu.make_async_copy(left, lf, local_sem.at[0]),
        pltpu.make_async_copy(right.at[0], rt, local_sem.at[1]),
        pltpu.make_async_copy(theta.at[0], vs.at[0], local_sem.at[2]),
    ]
    for load in loads:
        load.start()

    barrier = pltpu.get_barrier_semaphore()
    for d in range(1, n_seg):
        pl.semaphore_signal(barrier, inc=1, device_id={"seg": lax.rem(seg + d, n_seg)}, device_id_type=MESH)
    for d in range(1, n_sec):
        pl.semaphore_signal(barrier, inc=1, device_id={"sec": lax.rem(sec + d, n_sec)}, device_id_type=MESH)
    pl.semaphore_wait(barrier, n_seg + n_sec - 2)

    def m_copy(d):
        return pltpu.make_async_remote_copy(
            src_ref=maps.at[0], dst_ref=mp.at[seg], send_sem=m_send.at[d - 1], recv_sem=m_recv.at[seg],
            device_id={"seg": seg + d}, device_id_type=MESH,
        )

    def m_arrival(j):
        return pltpu.make_async_remote_copy(
            src_ref=maps.at[0], dst_ref=mp.at[j], send_sem=m_send.at[0], recv_sem=m_recv.at[j],
            device_id={"seg": j}, device_id_type=MESH,
        )

    def m_relay(j):
        other = seg + 1 - 2 * lax.rem(seg, 2)
        return pltpu.make_async_remote_copy(
            src_ref=mp.at[j], dst_ref=mp.at[j], send_sem=m_pass.at[j], recv_sem=m_recv.at[j],
            device_id={"seg": other}, device_id_type=MESH,
        )

    def m_direct(j):
        return (j < seg) & (lax.rem(seg + j, 2) == 0)

    def v_copy(t, source, side):
        other = sec - 1 if side == 0 else sec + 1
        return pltpu.make_async_remote_copy(
            src_ref=source, dst_ref=vh.at[t, 1 - side], send_sem=v_send.at[t, side],
            recv_sem=v_recv.at[t, 1 - side], device_id={"sec": other}, device_id_type=MESH,
        )

    def v_arrival(t, side):
        other = sec - 1 if side == 0 else sec + 1
        return pltpu.make_async_remote_copy(
            src_ref=vs.at[0, 0], dst_ref=vh.at[t, side], send_sem=v_send.at[t, side],
            recv_sem=v_recv.at[t, side], device_id={"sec": other}, device_id_type=MESH,
        )

    def r_copies(side):
        other = sec - 1 if side == 0 else sec + 1
        q, shift = (0, 1) if side == 0 else (blocks - 1, -1)
        return [
            pltpu.make_async_remote_copy(
                src_ref=right.at[0, w, q], dst_ref=rhalo.at[1 - side, i], send_sem=r_send.at[side, i],
                recv_sem=r_recv.at[1 - side, i], device_id={"sec": other}, device_id_type=MESH,
            )
            for i, w in enumerate(groups[shift])
        ]

    def r_arrivals(side):
        other = sec - 1 if side == 0 else sec + 1
        shift = -1 if side == 0 else 1
        return [
            pltpu.make_async_remote_copy(
                src_ref=right.at[0, w, 0], dst_ref=rhalo.at[side, i], send_sem=r_send.at[side, i],
                recv_sem=r_recv.at[side, i], device_id={"sec": other}, device_id_type=MESH,
            )
            for i, w in enumerate(groups[shift])
        ]

    def s_copy(stage, d):
        return pltpu.make_async_remote_copy(
            src_ref=red.at[stage, sec], dst_ref=red.at[stage, sec], send_sem=s_send.at[stage, d],
            recv_sem=s_recv.at[stage, sec], device_id={"sec": lax.rem(sec + d, n_sec)}, device_id_type=MESH,
        )

    def s_arrival(stage, d):
        other = lax.rem(sec + d, n_sec)
        return pltpu.make_async_remote_copy(
            src_ref=red.at[stage, sec], dst_ref=red.at[stage, other], send_sem=s_send.at[stage, d],
            recv_sem=s_recv.at[stage, other], device_id={"sec": other}, device_id_type=MESH,
        )

    def m_goes(d):
        return lax.rem(seg, 2) == 0 if d == 1 else seg + d < n_seg

    m_ways = [1] + list(range(2, n_seg, 2))
    for d in reversed(m_ways):
        @pl.when(m_goes(d))
        def _():
            m_copy(d).start()

    for side, there in ((0, has_low), (1, has_high)):
        q = 0 if side == 0 else blocks - 1
        @pl.when(there)
        def _():
            v_copy(0, theta.at[0, q], side).start()
            for copy in r_copies(side):
                copy.start()

        @pl.when(jnp.logical_not(there))
        def _():
            rhalo[side] = jnp.zeros_like(rhalo[side])
            for t in range(ITERS):
                vh[t, side] = jnp.zeros_like(vh[t, side])

    loads[0].wait()
    for q in range(blocks):
        for w in range(terms):
            l2[q, row[w] : row[w] + n, :] = wide(lf[w, q] * mask[q, w].astype(F32))
    loads[1].wait()
    for q in range(blocks):
        for d in (-1, 0, 1):
            if 0 <= q + d < blocks:
                for w in groups[d]:
                    r2[q, row[w] : row[w] + n, :] = wide(rt[w, q + d])
    loads[2].wait()

    for j in range(n_seg - 2):
        @pl.when(m_direct(j))
        def _():
            m_arrival(j).wait_recv()
            m_relay(j).start()

    @pl.when(seg == 0)
    def _():
        here = lax.broadcasted_iota(jnp.int32, (n, n), 0)
        across = lax.broadcasted_iota(jnp.int32, (n, n), 1)
        for q in range(blocks):
            amat[q] = (here == across).astype(F32)

    for j in range(n_seg - 1):
        @pl.when((j < seg) & jnp.logical_not(m_direct(j)))
        def _():
            m_arrival(j).wait_recv()

        @pl.when(j < seg)
        def _():
            for q in range(blocks):
                if j == 0:
                    amat[q] = mp[0, q]
                else:
                    amat[q] = halves(dot(wide(amat[q]), twice(mp[j, q])))

    for q in range(blocks):
        a = amat[q]
        turned = wide(a.T)
        doubled = twice(a)
        for d in (-1, 0, 1):
            for w in groups[d]:
                part = halves(dot(l2[q, row[w] : row[w] + n, :], doubled))
                l2[q, row[w] : row[w] + n, :] = wide(halves(dot(turned, twice(part))))

    def contribution(q, d, vector2):
        size = len(groups[d]) * n
        x = halves(dot(l2[q, start[d] : start[d] + size, :], vector2))
        x = jnp.concatenate([x[i * n : (i + 1) * n] for i in range(len(groups[d]))], axis=1)
        x = jnp.concatenate(split(x), axis=0)
        y = halves(dot(x, r2[q, start[d] : start[d] + size, :]))
        return y[:n] + y[n:]

    def step(t, _):
        own = [twice(vs[t, q]) for q in range(blocks)]
        image = []
        for q in range(blocks):
            total = None
            for d in (-1, 0, 1):
                if 0 <= q + d < blocks:
                    y = contribution(q, d, own[q + d])
                    total = y if total is None else total + y
            vs[t + 1, q] = total

        sides = ((0, has_low, 0, -1), (1, has_high, blocks - 1, 1))

        @pl.when(t == 0)
        def _():
            for side, there, q, d in sides:
                @pl.when(there)
                def _():
                    for copy in r_arrivals(side):
                        copy.wait_recv()

            for side, there, q, d in sides:
                for i, w in enumerate(groups[d]):
                    r2[q, row[w] : row[w] + n, :] = wide(rhalo[side, i])

        for side, there, q, d in sides:
            @pl.when(there)
            def _():
                v_arrival(t, side).wait_recv()

        crossed = [contribution(q, d, twice(vh[t, side])) for side, _, q, d in sides]
        for side, there, q, d in sides:
            vs[t + 1, q] = vs[t + 1, q] + crossed[side]
        for side, there, q, d in sides:
            @pl.when(there & (t < ITERS - 1))
            def _():
                v_copy(t + 1, vs.at[t + 1, q], side).start()

        @pl.when(t < ITERS - 1)
        def _():
            total = squares(vs[t + 1, 0])
            for q in range(1, blocks):
                total = total + squares(vs[t + 1, q])
            red[t // 2, sec, t % 2] = total

        @pl.when(t == 1)
        def _():
            for d in range(1, n_sec):
                s_copy(0, d).start()

        return 0

    lax.fori_loop(0, ITERS, step, 0)

    cells = n_sec * blocks * n * n

    def whole(stage):
        total = red[stage, 0]
        for other in range(1, n_sec):
            total = total + red[stage, other]
        first = jnp.sum(total[0], keepdims=True)
        second = jnp.sum(total[1], keepdims=True)
        return first / cells, second / cells

    for d in range(1, n_sec):
        s_arrival(0, d).wait_recv()
    m1, m2 = whole(0)
    s1 = lax.rsqrt(m1 + EPS)
    s12 = s1 * lax.rsqrt(s1 * s1 * m2 + EPS)
    last = [vs[ITERS, q] * s12 for q in range(blocks)]
    total = squares(last[0])
    for q in range(1, blocks):
        total = total + squares(last[q])
    red[1, sec, 1] = total
    for d in range(1, n_sec):
        s_copy(1, d).start()

    here = lax.broadcasted_iota(jnp.int32, (n, n), 0)
    across = lax.broadcasted_iota(jnp.int32, (n, n), 1)
    for q in range(blocks):
        theta_out[0, q] = last[q]
        kept = ((here < ranks[0, q]) & (across < ranks[0, q])).astype(F32)
        density[0, q] = halves(dot(wide(last[q]), twice(last[q].T))) * kept

    for d in range(1, n_sec):
        s_arrival(1, d).wait_recv()
    m3, m4 = whole(1)
    s3 = lax.rsqrt(s12 * s12 * m3 + EPS)
    s34 = s3 * lax.rsqrt(s3 * s3 * m4 + EPS)
    for q in range(blocks):
        theta_out[0, q] = theta_out[0, q] * s34
        density[0, q] = density[0, q] * (s34 * s34 / n)

    for d in m_ways:
        @pl.when(m_goes(d))
        def _():
            m_copy(d).wait_send()
    for j in range(n_seg - 2):
        @pl.when(m_direct(j))
        def _():
            m_relay(j).wait_send()
    for side, there in ((0, has_low), (1, has_high)):
        q = 0 if side == 0 else blocks - 1
        @pl.when(there)
        def _():
            v_copy(0, theta.at[0, q], side).wait_send()
            for t in range(1, ITERS):
                v_copy(t, vs.at[t, q], side).wait_send()
            for copy in r_copies(side):
                copy.wait_send()
    for stage in range(2):
        for d in range(1, n_sec):
            s_copy(stage, d).wait_send()


def place(theta, density, theta_out, density_out, sem):
    copies = [
        pltpu.make_async_copy(theta, theta_out, sem.at[0]),
        pltpu.make_async_copy(density, density_out, sem.at[1]),
    ]
    for copy in copies:
        copy.start()
    for copy in copies:
        copy.wait()


def per_device(n_seg, n_sec, theta_in, left_env, site_maps, right_env, mpo_mask, ranks):
    terms, blocks, n, _ = left_env.shape
    groups = {d: [w for w in range(terms) if w % 3 - 1 == d] for d in (-1, 0, 1)}
    most = max(len(g) for g in groups.values())
    block = (n, n)
    anywhere = pl.BlockSpec(memory_space=pl.ANY)
    scalars = pl.BlockSpec(memory_space=pltpu.SMEM)
    vmem = pl.BlockSpec(memory_space=pltpu.VMEM)
    out = jax.ShapeDtypeStruct(theta_in.shape, F32)
    dma = pltpu.SemaphoreType.DMA
    results = pl.pallas_call(
        functools.partial(kernel, n_seg, n_sec, groups),
        out_shape=(out, out),
        in_specs=[anywhere, anywhere, anywhere, anywhere, scalars, scalars],
        out_specs=(vmem, vmem),
        scratch_shapes=[
            pltpu.VMEM((terms, blocks) + block, F32),
            pltpu.VMEM((terms, blocks) + block, F32),
            pltpu.VMEM((n_seg, blocks) + block, F32),
            pltpu.VMEM((blocks,) + block, F32),
            pltpu.VMEM((2, most) + block, F32),
            pltpu.VMEM((ITERS, 2) + block, F32),
            pltpu.VMEM((ITERS + 1, blocks) + block, F32),
            pltpu.VMEM((blocks, terms * n, 2 * n), BF16),
            pltpu.VMEM((blocks, terms * n, 2 * n), BF16),
            pltpu.VMEM((2, n_sec, 2, 8, n), F32),
            dma((3,)),
            dma((n_seg,)),
            dma((n_seg,)),
            dma((n_seg,)),
            dma((2, most)),
            dma((2, most)),
            dma((ITERS, 2)),
            dma((ITERS, 2)),
            dma((2, n_sec)),
            dma((2, n_sec)),
        ],
        compiler_params=pltpu.CompilerParams(
            collective_id=0, has_side_effects=True
        ),
        cost_estimate=pl.CostEstimate(flops=2 * n**3 * 4 * 200, bytes_accessed=4 * n * n * 60, transcendentals=0),
    )(theta_in, left_env, site_maps, right_env, mpo_mask.T, ranks)
    return pl.pallas_call(
        place,
        out_shape=(out, out),
        in_specs=[anywhere, anywhere],
        out_specs=(anywhere, anywhere),
        scratch_shapes=[dma((2,))],
    )(*results)


def solution(mesh):
    n_seg, n_sec = mesh.shape["seg"], mesh.shape["sec"]
    return jax.shard_map(
        functools.partial(per_device, n_seg, n_sec),
        mesh=mesh,
        in_specs=(
            P("seg", "sec", None, None),
            P(None, "sec", None, None),
            P("seg", "sec", None, None),
            P("seg", None, "sec", None, None),
            P(None, "sec"),
            P("seg", "sec"),
        ),
        out_specs=(P("seg", "sec", None, None), P("seg", "sec", None, None)),
        check_vma=False,
    )
```

```python
import functools

import jax
import jax.numpy as jnp
from jax import lax
from jax.experimental import pallas as pl
from jax.experimental.pallas import tpu as pltpu
from jax.sharding import PartitionSpec as P

ITERS = 4
EPS = 1e-06
MESH = pl.DeviceIdType.MESH
F32, BF16 = jnp.float32, jnp.bfloat16


def split(x):
    high = x.astype(BF16)
    low = (x - high.astype(F32)).astype(BF16)
    return high, low


def wide(x):
    return jnp.concatenate(split(x), axis=1)


def twice(x):
    pair = wide(x)
    return jnp.concatenate([pair, pair], axis=0)


def dot(a, b):
    return lax.dot_general(a, b, (((1,), (0,)), ((), ())), preferred_element_type=F32)


def halves(x):
    n = x.shape[1] // 2
    return x[:, :n] + x[:, n:]


def squares(x):
    return jnp.sum((x * x).reshape(-1, 8, x.shape[1]), axis=0)


def kernel(
    n_seg, n_sec, groups, theta, left, maps, right, mask, ranks, theta_out, density,
    lf, rt, mp, amat, rhalo, vh, vs, l2, r2, red,
    local_sem, m_send, m_recv, m_pass, r_send, r_recv, v_send, v_recv, s_send, s_recv,
):
    seg, sec = lax.axis_index("seg"), lax.axis_index("sec")
    blocks, n = theta.shape[1], theta.shape[2]
    terms = left.shape[0]
    has_low, has_high = sec > 0, sec < n_sec - 1
    row = {}
    start = {}
    for d in (-1, 0, 1):
        start[d] = len(row) * n
        for w in groups[d]:
            row[w] = len(row) * n

    loads = [
        pltpu.make_async_copy(left, lf, local_sem.at[0]),
        pltpu.make_async_copy(right.at[0], rt, local_sem.at[1]),
        pltpu.make_async_copy(theta.at[0], vs.at[0], local_sem.at[2]),
    ]
    for load in loads:
        load.start()

    barrier = pltpu.get_barrier_semaphore()
    for d in range(1, n_seg):
        pl.semaphore_signal(barrier, inc=1, device_id={"seg": lax.rem(seg + d, n_seg)}, device_id_type=MESH)
    for d in range(1, n_sec):
        pl.semaphore_signal(barrier, inc=1, device_id={"sec": lax.rem(sec + d, n_sec)}, device_id_type=MESH)
    pl.semaphore_wait(barrier, n_seg + n_sec - 2)

    def m_copy(d):
        return pltpu.make_async_remote_copy(
            src_ref=maps.at[0], dst_ref=mp.at[seg], send_sem=m_send.at[d - 1], recv_sem=m_recv.at[seg],
            device_id={"seg": seg + d}, device_id_type=MESH,
        )

    def m_arrival(j):
        return pltpu.make_async_remote_copy(
            src_ref=maps.at[0], dst_ref=mp.at[j], send_sem=m_send.at[0], recv_sem=m_recv.at[j],
            device_id={"seg": j}, device_id_type=MESH,
        )

    def m_relay(j):
        other = seg + 1 - 2 * lax.rem(seg, 2)
        return pltpu.make_async_remote_copy(
            src_ref=mp.at[j], dst_ref=mp.at[j], send_sem=m_pass.at[j], recv_sem=m_recv.at[j],
            device_id={"seg": other}, device_id_type=MESH,
        )

    def m_direct(j):
        return (j < seg) & (lax.rem(seg + j, 2) == 0)

    def v_copy(t, source, side):
        other = sec - 1 if side == 0 else sec + 1
        return pltpu.make_async_remote_copy(
            src_ref=source, dst_ref=vh.at[t, 1 - side], send_sem=v_send.at[t, side],
            recv_sem=v_recv.at[t, 1 - side], device_id={"sec": other}, device_id_type=MESH,
        )

    def v_arrival(t, side):
        other = sec - 1 if side == 0 else sec + 1
        return pltpu.make_async_remote_copy(
            src_ref=vs.at[0, 0], dst_ref=vh.at[t, side], send_sem=v_send.at[t, side],
            recv_sem=v_recv.at[t, side], device_id={"sec": other}, device_id_type=MESH,
        )

    def r_copies(side):
        other = sec - 1 if side == 0 else sec + 1
        q, shift = (0, 1) if side == 0 else (blocks - 1, -1)
        return [
            pltpu.make_async_remote_copy(
                src_ref=right.at[0, w, q], dst_ref=rhalo.at[1 - side, i], send_sem=r_send.at[side, i],
                recv_sem=r_recv.at[1 - side, i], device_id={"sec": other}, device_id_type=MESH,
            )
            for i, w in enumerate(groups[shift])
        ]

    def r_arrivals(side):
        other = sec - 1 if side == 0 else sec + 1
        shift = -1 if side == 0 else 1
        return [
            pltpu.make_async_remote_copy(
                src_ref=right.at[0, w, 0], dst_ref=rhalo.at[side, i], send_sem=r_send.at[side, i],
                recv_sem=r_recv.at[side, i], device_id={"sec": other}, device_id_type=MESH,
            )
            for i, w in enumerate(groups[shift])
        ]

    def s_copy(stage, d):
        return pltpu.make_async_remote_copy(
            src_ref=red.at[stage, sec], dst_ref=red.at[stage, sec], send_sem=s_send.at[stage, d],
            recv_sem=s_recv.at[stage, sec], device_id={"sec": lax.rem(sec + d, n_sec)}, device_id_type=MESH,
        )

    def s_arrival(stage, d):
        other = lax.rem(sec + d, n_sec)
        return pltpu.make_async_remote_copy(
            src_ref=red.at[stage, sec], dst_ref=red.at[stage, other], send_sem=s_send.at[stage, d],
            recv_sem=s_recv.at[stage, other], device_id={"sec": other}, device_id_type=MESH,
        )

    def m_goes(d):
        return lax.rem(seg, 2) == 0 if d == 1 else seg + d < n_seg

    m_ways = [1] + list(range(2, n_seg, 2))
    for d in reversed(m_ways):
        @pl.when(m_goes(d))
        def _():
            m_copy(d).start()

    for side, there in ((0, has_low), (1, has_high)):
        q = 0 if side == 0 else blocks - 1
        @pl.when(there)
        def _():
            v_copy(0, theta.at[0, q], side).start()
            for copy in r_copies(side):
                copy.start()

        @pl.when(jnp.logical_not(there))
        def _():
            rhalo[side] = jnp.zeros_like(rhalo[side])
            for t in range(ITERS):
                vh[t, side] = jnp.zeros_like(vh[t, side])

    loads[0].wait()
    for q in range(blocks):
        for w in range(terms):
            l2[q, row[w] : row[w] + n, :] = wide(lf[w, q] * mask[q, w].astype(F32))
    loads[1].wait()
    for q in range(blocks):
        for d in (-1, 0, 1):
            if 0 <= q + d < blocks:
                for w in groups[d]:
                    r2[q, row[w] : row[w] + n, :] = wide(rt[w, q + d])
    loads[2].wait()

    for j in range(n_seg - 2):
        @pl.when(m_direct(j))
        def _():
            m_arrival(j).wait_recv()
            m_relay(j).start()

    @pl.when(seg == 0)
    def _():
        here = lax.broadcasted_iota(jnp.int32, (n, n), 0)
        across = lax.broadcasted_iota(jnp.int32, (n, n), 1)
        for q in range(blocks):
            amat[q] = (here == across).astype(F32)

    for j in range(n_seg - 1):
        @pl.when((j < seg) & jnp.logical_not(m_direct(j)))
        def _():
            m_arrival(j).wait_recv()

        @pl.when(j < seg)
        def _():
            for q in range(blocks):
                if j == 0:
                    amat[q] = mp[0, q]
                else:
                    amat[q] = halves(dot(wide(amat[q]), twice(mp[j, q])))

    for q in range(blocks):
        a = amat[q]
        turned = wide(a.T)
        doubled = twice(a)
        for d in (-1, 0, 1):
            for w in groups[d]:
                part = halves(dot(l2[q, row[w] : row[w] + n, :], doubled))
                l2[q, row[w] : row[w] + n, :] = wide(halves(dot(turned, twice(part))))

    def contribution(q, d, vector2):
        size = len(groups[d]) * n
        x = halves(dot(l2[q, start[d] : start[d] + size, :], vector2))
        x = jnp.concatenate([x[i * n : (i + 1) * n] for i in range(len(groups[d]))], axis=1)
        x = jnp.concatenate(split(x), axis=0)
        y = halves(dot(x, r2[q, start[d] : start[d] + size, :]))
        return y[:n] + y[n:]

    def step(t, _):
        own = [twice(vs[t, q]) for q in range(blocks)]
        image = []
        for q in range(blocks):
            total = None
            for d in (-1, 0, 1):
                if 0 <= q + d < blocks:
                    y = contribution(q, d, own[q + d])
                    total = y if total is None else total + y
            vs[t + 1, q] = total

        sides = ((0, has_low, 0, -1), (1, has_high, blocks - 1, 1))

        @pl.when(t == 0)
        def _():
            for side, there, q, d in sides:
                @pl.when(there)
                def _():
                    for copy in r_arrivals(side):
                        copy.wait_recv()

            for side, there, q, d in sides:
                for i, w in enumerate(groups[d]):
                    r2[q, row[w] : row[w] + n, :] = wide(rhalo[side, i])

        for side, there, q, d in sides:
            @pl.when(there)
            def _():
                v_arrival(t, side).wait_recv()

        crossed = [contribution(q, d, twice(vh[t, side])) for side, _, q, d in sides]
        for side, there, q, d in sides:
            vs[t + 1, q] = vs[t + 1, q] + crossed[side]
        for side, there, q, d in sides:
            @pl.when(there & (t < ITERS - 1))
            def _():
                v_copy(t + 1, vs.at[t + 1, q], side).start()

        @pl.when(t < ITERS - 1)
        def _():
            total = squares(vs[t + 1, 0])
            for q in range(1, blocks):
                total = total + squares(vs[t + 1, q])
            red[t // 2, sec, t % 2] = total

        @pl.when(t == 1)
        def _():
            for d in range(1, n_sec):
                s_copy(0, d).start()

        return 0

    lax.fori_loop(0, ITERS, step, 0)

    cells = n_sec * blocks * n * n

    def whole(stage):
        total = red[stage, 0]
        for other in range(1, n_sec):
            total = total + red[stage, other]
        first = jnp.sum(total[0], keepdims=True)
        second = jnp.sum(total[1], keepdims=True)
        return first / cells, second / cells

    for d in range(1, n_sec):
        s_arrival(0, d).wait_recv()
    m1, m2 = whole(0)
    s1 = lax.rsqrt(m1 + EPS)
    s12 = s1 * lax.rsqrt(s1 * s1 * m2 + EPS)
    last = [vs[ITERS, q] * s12 for q in range(blocks)]
    total = squares(last[0])
    for q in range(1, blocks):
        total = total + squares(last[q])
    red[1, sec, 1] = total
    for d in range(1, n_sec):
        s_copy(1, d).start()

    here = lax.broadcasted_iota(jnp.int32, (n, n), 0)
    across = lax.broadcasted_iota(jnp.int32, (n, n), 1)
    for q in range(blocks):
        theta_out[0, q] = last[q]
        kept = ((here < ranks[0, q]) & (across < ranks[0, q])).astype(F32)
        density[0, q] = halves(dot(wide(last[q]), twice(last[q].T))) * kept

    for d in range(1, n_sec):
        s_arrival(1, d).wait_recv()
    m3, m4 = whole(1)
    s3 = lax.rsqrt(s12 * s12 * m3 + EPS)
    s34 = s3 * lax.rsqrt(s3 * s3 * m4 + EPS)
    for q in range(blocks):
        theta_out[0, q] = theta_out[0, q] * s34
        density[0, q] = density[0, q] * (s34 * s34 / n)

    for d in m_ways:
        @pl.when(m_goes(d))
        def _():
            m_copy(d).wait_send()
    for j in range(n_seg - 2):
        @pl.when(m_direct(j))
        def _():
            m_relay(j).wait_send()
    for side, there in ((0, has_low), (1, has_high)):
        q = 0 if side == 0 else blocks - 1
        @pl.when(there)
        def _():
            v_copy(0, theta.at[0, q], side).wait_send()
            for t in range(1, ITERS):
                v_copy(t, vs.at[t, q], side).wait_send()
            for copy in r_copies(side):
                copy.wait_send()
    for stage in range(2):
        for d in range(1, n_sec):
            s_copy(stage, d).wait_send()


def place(theta, density, theta_out, density_out, held, sem):
    arrays = ((theta, theta_out), (density, density_out))
    arrivals = [pltpu.make_async_copy(a, held.at[i], sem.at[0, i]) for i, (a, _) in enumerate(arrays)]
    departures = [pltpu.make_async_copy(held.at[i], b, sem.at[1, i]) for i, (_, b) in enumerate(arrays)]
    for copy in arrivals:
        copy.start()
    for arrival, departure in zip(arrivals, departures):
        arrival.wait()
        departure.start()
    for copy in departures:
        copy.wait()


def per_device(n_seg, n_sec, theta_in, left_env, site_maps, right_env, mpo_mask, ranks):
    terms, blocks, n, _ = left_env.shape
    groups = {d: [w for w in range(terms) if w % 3 - 1 == d] for d in (-1, 0, 1)}
    most = max(len(g) for g in groups.values())
    block = (n, n)
    anywhere = pl.BlockSpec(memory_space=pl.ANY)
    scalars = pl.BlockSpec(memory_space=pltpu.SMEM)
    vmem = pl.BlockSpec(memory_space=pltpu.VMEM)
    out = jax.ShapeDtypeStruct(theta_in.shape, F32)
    dma = pltpu.SemaphoreType.DMA
    results = pl.pallas_call(
        functools.partial(kernel, n_seg, n_sec, groups),
        out_shape=(out, out),
        in_specs=[anywhere, anywhere, anywhere, anywhere, scalars, scalars],
        out_specs=(vmem, vmem),
        scratch_shapes=[
            pltpu.VMEM((terms, blocks) + block, F32),
            pltpu.VMEM((terms, blocks) + block, F32),
            pltpu.VMEM((n_seg, blocks) + block, F32),
            pltpu.VMEM((blocks,) + block, F32),
            pltpu.VMEM((2, most) + block, F32),
            pltpu.VMEM((ITERS, 2) + block, F32),
            pltpu.VMEM((ITERS + 1, blocks) + block, F32),
            pltpu.VMEM((blocks, terms * n, 2 * n), BF16),
            pltpu.VMEM((blocks, terms * n, 2 * n), BF16),
            pltpu.VMEM((2, n_sec, 2, 8, n), F32),
            dma((3,)),
            dma((n_seg,)),
            dma((n_seg,)),
            dma((n_seg,)),
            dma((2, most)),
            dma((2, most)),
            dma((ITERS, 2)),
            dma((ITERS, 2)),
            dma((2, n_sec)),
            dma((2, n_sec)),
        ],
        compiler_params=pltpu.CompilerParams(
            collective_id=0, has_side_effects=True
        ),
        cost_estimate=pl.CostEstimate(flops=2 * n**3 * 4 * 200, bytes_accessed=4 * n * n * 60, transcendentals=0),
    )(theta_in, left_env, site_maps, right_env, mpo_mask.T, ranks)
    return pl.pallas_call(
        place,
        out_shape=(out, out),
        in_specs=[anywhere, anywhere],
        out_specs=(anywhere, anywhere),
        scratch_shapes=[pltpu.VMEM((2,) + theta_in.shape, F32), dma((2, 2))],
    )(*results)


def solution(mesh):
    n_seg, n_sec = mesh.shape["seg"], mesh.shape["sec"]
    return jax.shard_map(
        functools.partial(per_device, n_seg, n_sec),
        mesh=mesh,
        in_specs=(
            P("seg", "sec", None, None),
            P(None, "sec", None, None),
            P("seg", "sec", None, None),
            P("seg", None, "sec", None, None),
            P(None, "sec"),
            P("seg", "sec"),
        ),
        out_specs=(P("seg", "sec", None, None), P("seg", "sec", None, None)),
        check_vma=False,
    )
```

```python
import functools

import jax
import jax.numpy as jnp
from jax import lax
from jax.experimental import pallas as pl
from jax.experimental.pallas import tpu as pltpu
from jax.sharding import PartitionSpec as P

ITERS = 4
EPS = 1e-06
MESH = pl.DeviceIdType.MESH
F32, BF16 = jnp.float32, jnp.bfloat16


def split(x):
    high = x.astype(BF16)
    low = (x - high.astype(F32)).astype(BF16)
    return high, low


def wide(x):
    return jnp.concatenate(split(x), axis=1)


def twice(x):
    pair = wide(x)
    return jnp.concatenate([pair, pair], axis=0)


def dot(a, b):
    return lax.dot_general(a, b, (((1,), (0,)), ((), ())), preferred_element_type=F32)


def halves(x):
    n = x.shape[1] // 2
    return x[:, :n] + x[:, n:]


def squares(x):
    return jnp.sum((x * x).reshape(-1, 8, x.shape[1]), axis=0)


def kernel(
    n_seg, n_sec, groups, theta, left, maps, right, mask, ranks, theta_out, density,
    lf, rt, mp, amat, rhalo, vh, vs, l2, r2, red, scale,
    local_sem, m_send, m_recv, m_pass, r_send, r_recv, v_send, v_recv, s_send, s_recv,
):
    seg, sec = lax.axis_index("seg"), lax.axis_index("sec")
    blocks, n = theta.shape[1], theta.shape[2]
    terms = left.shape[0]
    has_low, has_high = sec > 0, sec < n_sec - 1
    row = {}
    start = {}
    for d in (-1, 0, 1):
        start[d] = len(row) * n
        for w in groups[d]:
            row[w] = len(row) * n

    loads = [
        pltpu.make_async_copy(left, lf, local_sem.at[0]),
        pltpu.make_async_copy(right.at[0], rt, local_sem.at[1]),
        pltpu.make_async_copy(theta.at[0], vs.at[0], local_sem.at[2]),
    ]
    for load in loads:
        load.start()

    barrier = pltpu.get_barrier_semaphore()
    for d in range(1, n_seg):
        pl.semaphore_signal(barrier, inc=1, device_id={"seg": lax.rem(seg + d, n_seg)}, device_id_type=MESH)
    for d in range(1, n_sec):
        pl.semaphore_signal(barrier, inc=1, device_id={"sec": lax.rem(sec + d, n_sec)}, device_id_type=MESH)
    pl.semaphore_wait(barrier, n_seg + n_sec - 2)

    def m_copy(d):
        return pltpu.make_async_remote_copy(
            src_ref=maps.at[0], dst_ref=mp.at[seg], send_sem=m_send.at[d - 1], recv_sem=m_recv.at[seg],
            device_id={"seg": seg + d}, device_id_type=MESH,
        )

    def m_arrival(j):
        return pltpu.make_async_remote_copy(
            src_ref=maps.at[0], dst_ref=mp.at[j], send_sem=m_send.at[0], recv_sem=m_recv.at[j],
            device_id={"seg": j}, device_id_type=MESH,
        )

    def m_relay(j):
        other = seg + 1 - 2 * lax.rem(seg, 2)
        return pltpu.make_async_remote_copy(
            src_ref=mp.at[j], dst_ref=mp.at[j], send_sem=m_pass.at[j], recv_sem=m_recv.at[j],
            device_id={"seg": other}, device_id_type=MESH,
        )

    def m_direct(j):
        return (j < seg) & (lax.rem(seg + j, 2) == 0)

    def v_copy(t, source, side):
        other = sec - 1 if side == 0 else sec + 1
        return pltpu.make_async_remote_copy(
            src_ref=source, dst_ref=vh.at[t, 1 - side], send_sem=v_send.at[t, side],
            recv_sem=v_recv.at[t, 1 - side], device_id={"sec": other}, device_id_type=MESH,
        )

    def v_arrival(t, side):
        other = sec - 1 if side == 0 else sec + 1
        return pltpu.make_async_remote_copy(
            src_ref=vs.at[0, 0], dst_ref=vh.at[t, side], send_sem=v_send.at[t, side],
            recv_sem=v_recv.at[t, side], device_id={"sec": other}, device_id_type=MESH,
        )

    def r_copies(side):
        other = sec - 1 if side == 0 else sec + 1
        q, shift = (0, 1) if side == 0 else (blocks - 1, -1)
        return [
            pltpu.make_async_remote_copy(
                src_ref=right.at[0, w, q], dst_ref=rhalo.at[1 - side, i], send_sem=r_send.at[side, i],
                recv_sem=r_recv.at[1 - side, i], device_id={"sec": other}, device_id_type=MESH,
            )
            for i, w in enumerate(groups[shift])
        ]

    def r_arrivals(side):
        other = sec - 1 if side == 0 else sec + 1
        shift = -1 if side == 0 else 1
        return [
            pltpu.make_async_remote_copy(
                src_ref=right.at[0, w, 0], dst_ref=rhalo.at[side, i], send_sem=r_send.at[side, i],
                recv_sem=r_recv.at[side, i], device_id={"sec": other}, device_id_type=MESH,
            )
            for i, w in enumerate(groups[shift])
        ]

    def s_copy(stage, d):
        return pltpu.make_async_remote_copy(
            src_ref=red.at[stage, sec], dst_ref=red.at[stage, sec], send_sem=s_send.at[stage, d],
            recv_sem=s_recv.at[stage, sec], device_id={"sec": lax.rem(sec + d, n_sec)}, device_id_type=MESH,
        )

    def s_arrival(stage, d):
        other = lax.rem(sec + d, n_sec)
        return pltpu.make_async_remote_copy(
            src_ref=red.at[stage, sec], dst_ref=red.at[stage, other], send_sem=s_send.at[stage, d],
            recv_sem=s_recv.at[stage, other], device_id={"sec": other}, device_id_type=MESH,
        )

    def m_goes(d):
        return lax.rem(seg, 2) == 0 if d == 1 else seg + d < n_seg

    m_ways = [1] + list(range(2, n_seg, 2))
    for d in reversed(m_ways):
        @pl.when(m_goes(d))
        def _():
            m_copy(d).start()

    for side, there in ((0, has_low), (1, has_high)):
        q = 0 if side == 0 else blocks - 1
        @pl.when(there)
        def _():
            v_copy(0, theta.at[0, q], side).start()
            for copy in r_copies(side):
                copy.start()

        @pl.when(jnp.logical_not(there))
        def _():
            rhalo[side] = jnp.zeros_like(rhalo[side])
            for t in range(ITERS):
                vh[t, side] = jnp.zeros_like(vh[t, side])

    loads[0].wait()
    for q in range(blocks):
        for w in range(terms):
            l2[q, row[w] : row[w] + n, :] = wide(lf[w, q] * mask[q, w].astype(F32))
    loads[1].wait()
    for q in range(blocks):
        for d in (-1, 0, 1):
            if 0 <= q + d < blocks:
                for w in groups[d]:
                    r2[q, row[w] : row[w] + n, :] = wide(rt[w, q + d])
    loads[2].wait()

    for j in range(n_seg - 2):
        @pl.when(m_direct(j))
        def _():
            m_arrival(j).wait_recv()
            m_relay(j).start()

    @pl.when(seg == 0)
    def _():
        here = lax.broadcasted_iota(jnp.int32, (n, n), 0)
        across = lax.broadcasted_iota(jnp.int32, (n, n), 1)
        for q in range(blocks):
            amat[q] = (here == across).astype(F32)

    for j in range(n_seg - 1):
        @pl.when((j < seg) & jnp.logical_not(m_direct(j)))
        def _():
            m_arrival(j).wait_recv()

        @pl.when(j < seg)
        def _():
            for q in range(blocks):
                if j == 0:
                    amat[q] = mp[0, q]
                else:
                    amat[q] = halves(dot(wide(amat[q]), twice(mp[j, q])))

    for q in range(blocks):
        a = amat[q]
        turned = wide(a.T)
        doubled = twice(a)
        for d in (-1, 0, 1):
            for w in groups[d]:
                part = halves(dot(l2[q, row[w] : row[w] + n, :], doubled))
                l2[q, row[w] : row[w] + n, :] = wide(halves(dot(turned, twice(part))))

    def contribution(q, d, vector2):
        size = len(groups[d]) * n
        x = halves(dot(l2[q, start[d] : start[d] + size, :], vector2))
        x = jnp.concatenate([x[i * n : (i + 1) * n] for i in range(len(groups[d]))], axis=1)
        x = jnp.concatenate(split(x), axis=0)
        y = halves(dot(x, r2[q, start[d] : start[d] + size, :]))
        return y[:n] + y[n:]

    cells = n_sec * blocks * n * n

    def whole(stage):
        total = red[stage, 0]
        for other in range(1, n_sec):
            total = total + red[stage, other]
        first = jnp.sum(total[0], keepdims=True)
        second = jnp.sum(total[1], keepdims=True)
        return first / cells, second / cells

    def step(t, _):
        own = [twice(vs[t, q]) for q in range(blocks)]
        image = []
        for q in range(blocks):
            total = None
            for d in (-1, 0, 1):
                if 0 <= q + d < blocks:
                    y = contribution(q, d, own[q + d])
                    total = y if total is None else total + y
            vs[t + 1, q] = total

        @pl.when(t == ITERS - 1)
        def _():
            for d in range(1, n_sec):
                s_arrival(0, d).wait_recv()
            m1, m2 = whole(0)
            s1 = lax.rsqrt(m1 + EPS)
            scale[...] = jnp.broadcast_to(s1 * lax.rsqrt(s1 * s1 * m2 + EPS), scale.shape)

        sides = ((0, has_low, 0, -1), (1, has_high, blocks - 1, 1))

        @pl.when(t == 0)
        def _():
            for side, there, q, d in sides:
                @pl.when(there)
                def _():
                    for copy in r_arrivals(side):
                        copy.wait_recv()

            for side, there, q, d in sides:
                for i, w in enumerate(groups[d]):
                    r2[q, row[w] : row[w] + n, :] = wide(rhalo[side, i])

        for side, there, q, d in sides:
            @pl.when(there)
            def _():
                v_arrival(t, side).wait_recv()

        crossed = [contribution(q, d, twice(vh[t, side])) for side, _, q, d in sides]
        for side, there, q, d in sides:
            vs[t + 1, q] = vs[t + 1, q] + crossed[side]
        for side, there, q, d in sides:
            @pl.when(there & (t < ITERS - 1))
            def _():
                v_copy(t + 1, vs.at[t + 1, q], side).start()

        @pl.when(t < ITERS - 1)
        def _():
            total = squares(vs[t + 1, 0])
            for q in range(1, blocks):
                total = total + squares(vs[t + 1, q])
            red[t // 2, sec, t % 2] = total

        @pl.when(t == 1)
        def _():
            for d in range(1, n_sec):
                s_copy(0, d).start()

        return 0

    lax.fori_loop(0, ITERS, step, 0)

    s12 = scale[0:1, :]
    last = [vs[ITERS, q] * s12 for q in range(blocks)]
    total = squares(last[0])
    for q in range(1, blocks):
        total = total + squares(last[q])
    red[1, sec, 1] = total
    for d in range(1, n_sec):
        s_copy(1, d).start()

    here = lax.broadcasted_iota(jnp.int32, (n, n), 0)
    across = lax.broadcasted_iota(jnp.int32, (n, n), 1)
    for q in range(blocks):
        theta_out[0, q] = last[q]
        kept = ((here < ranks[0, q]) & (across < ranks[0, q])).astype(F32)
        density[0, q] = halves(dot(wide(last[q]), twice(last[q].T))) * kept

    for d in range(1, n_sec):
        s_arrival(1, d).wait_recv()
    m3, m4 = whole(1)
    s3 = lax.rsqrt(s12 * s12 * m3 + EPS)
    s34 = s3 * lax.rsqrt(s3 * s3 * m4 + EPS)
    for q in range(blocks):
        theta_out[0, q] = theta_out[0, q] * s34
        density[0, q] = density[0, q] * (s34 * s34 / n)

    for d in m_ways:
        @pl.when(m_goes(d))
        def _():
            m_copy(d).wait_send()
    for j in range(n_seg - 2):
        @pl.when(m_direct(j))
        def _():
            m_relay(j).wait_send()
    for side, there in ((0, has_low), (1, has_high)):
        q = 0 if side == 0 else blocks - 1
        @pl.when(there)
        def _():
            v_copy(0, theta.at[0, q], side).wait_send()
            for t in range(1, ITERS):
                v_copy(t, vs.at[t, q], side).wait_send()
            for copy in r_copies(side):
                copy.wait_send()
    for stage in range(2):
        for d in range(1, n_sec):
            s_copy(stage, d).wait_send()


def place(theta, density, theta_out, density_out, held, sem):
    arrays = ((theta, theta_out), (density, density_out))
    arrivals = [pltpu.make_async_copy(a, held.at[i], sem.at[0, i]) for i, (a, _) in enumerate(arrays)]
    departures = [pltpu.make_async_copy(held.at[i], b, sem.at[1, i]) for i, (_, b) in enumerate(arrays)]
    for copy in arrivals:
        copy.start()
    for arrival, departure in zip(arrivals, departures):
        arrival.wait()
        departure.start()
    for copy in departures:
        copy.wait()


def per_device(n_seg, n_sec, theta_in, left_env, site_maps, right_env, mpo_mask, ranks):
    terms, blocks, n, _ = left_env.shape
    groups = {d: [w for w in range(terms) if w % 3 - 1 == d] for d in (-1, 0, 1)}
    most = max(len(g) for g in groups.values())
    block = (n, n)
    anywhere = pl.BlockSpec(memory_space=pl.ANY)
    scalars = pl.BlockSpec(memory_space=pltpu.SMEM)
    vmem = pl.BlockSpec(memory_space=pltpu.VMEM)
    out = jax.ShapeDtypeStruct(theta_in.shape, F32)
    dma = pltpu.SemaphoreType.DMA
    results = pl.pallas_call(
        functools.partial(kernel, n_seg, n_sec, groups),
        out_shape=(out, out),
        in_specs=[anywhere, anywhere, anywhere, anywhere, scalars, scalars],
        out_specs=(vmem, vmem),
        scratch_shapes=[
            pltpu.VMEM((terms, blocks) + block, F32),
            pltpu.VMEM((terms, blocks) + block, F32),
            pltpu.VMEM((n_seg, blocks) + block, F32),
            pltpu.VMEM((blocks,) + block, F32),
            pltpu.VMEM((2, most) + block, F32),
            pltpu.VMEM((ITERS, 2) + block, F32),
            pltpu.VMEM((ITERS + 1, blocks) + block, F32),
            pltpu.VMEM((blocks, terms * n, 2 * n), BF16),
            pltpu.VMEM((blocks, terms * n, 2 * n), BF16),
            pltpu.VMEM((2, n_sec, 2, 8, n), F32),
            pltpu.VMEM((8, n), F32),
            dma((3,)),
            dma((n_seg,)),
            dma((n_seg,)),
            dma((n_seg,)),
            dma((2, most)),
            dma((2, most)),
            dma((ITERS, 2)),
            dma((ITERS, 2)),
            dma((2, n_sec)),
            dma((2, n_sec)),
        ],
        compiler_params=pltpu.CompilerParams(
            collective_id=0, has_side_effects=True
        ),
        cost_estimate=pl.CostEstimate(flops=2 * n**3 * 4 * 200, bytes_accessed=4 * n * n * 60, transcendentals=0),
    )(theta_in, left_env, site_maps, right_env, mpo_mask.T, ranks)
    return pl.pallas_call(
        place,
        out_shape=(out, out),
        in_specs=[anywhere, anywhere],
        out_specs=(anywhere, anywhere),
        scratch_shapes=[pltpu.VMEM((2,) + theta_in.shape, F32), dma((2, 2))],
    )(*results)


def solution(mesh):
    n_seg, n_sec = mesh.shape["seg"], mesh.shape["sec"]
    return jax.shard_map(
        functools.partial(per_device, n_seg, n_sec),
        mesh=mesh,
        in_specs=(
            P("seg", "sec", None, None),
            P(None, "sec", None, None),
            P("seg", "sec", None, None),
            P("seg", None, "sec", None, None),
            P(None, "sec"),
            P("seg", "sec"),
        ),
        out_specs=(P("seg", "sec", None, None), P("seg", "sec", None, None)),
        check_vma=False,
    )
```

```python
import functools

import jax
import jax.numpy as jnp
from jax import lax
from jax.experimental import pallas as pl
from jax.experimental.pallas import tpu as pltpu
from jax.sharding import PartitionSpec as P

ITERS = 4
EPS = 1e-06
MESH = pl.DeviceIdType.MESH
F32, BF16 = jnp.float32, jnp.bfloat16


def split(x):
    high = x.astype(BF16)
    low = (x - high.astype(F32)).astype(BF16)
    return high, low


def wide(x):
    return jnp.concatenate(split(x), axis=1)


def twice(x):
    pair = wide(x)
    return jnp.concatenate([pair, pair], axis=0)


def dot(a, b):
    return lax.dot_general(a, b, (((1,), (0,)), ((), ())), preferred_element_type=F32)


def halves(x):
    n = x.shape[1] // 2
    return x[:, :n] + x[:, n:]


def squares(x):
    return jnp.sum((x * x).reshape(-1, 8, x.shape[1]), axis=0)


def kernel(
    n_seg, n_sec, groups, theta, left, maps, right, mask, ranks, theta_out, density,
    lf, rt, mp, amat, rhalo, vh, vs, l2, r2, red, scale,
    local_sem, m_send, m_recv, m_pass, r_send, r_recv, v_send, v_recv, s_send, s_recv,
):
    seg, sec = lax.axis_index("seg"), lax.axis_index("sec")
    blocks, n = theta.shape[1], theta.shape[2]
    terms = left.shape[0]
    has_low, has_high = sec > 0, sec < n_sec - 1
    row = {}
    start = {}
    for d in (-1, 0, 1):
        start[d] = len(row) * n
        for w in groups[d]:
            row[w] = len(row) * n

    loads = [
        pltpu.make_async_copy(left, lf, local_sem.at[0]),
        pltpu.make_async_copy(right.at[0], rt, local_sem.at[1]),
        pltpu.make_async_copy(theta.at[0], vs.at[0], local_sem.at[2]),
    ]
    for load in loads:
        load.start()

    barrier = pltpu.get_barrier_semaphore()
    for d in range(1, n_seg):
        pl.semaphore_signal(barrier, inc=1, device_id={"seg": lax.rem(seg + d, n_seg)}, device_id_type=MESH)
    for d in range(1, n_sec):
        pl.semaphore_signal(barrier, inc=1, device_id={"sec": lax.rem(sec + d, n_sec)}, device_id_type=MESH)
    pl.semaphore_wait(barrier, n_seg + n_sec - 2)

    def m_copy(d):
        return pltpu.make_async_remote_copy(
            src_ref=maps.at[0], dst_ref=mp.at[seg], send_sem=m_send.at[d - 1], recv_sem=m_recv.at[seg],
            device_id={"seg": seg + d}, device_id_type=MESH,
        )

    def m_arrival(j):
        return pltpu.make_async_remote_copy(
            src_ref=maps.at[0], dst_ref=mp.at[j], send_sem=m_send.at[0], recv_sem=m_recv.at[j],
            device_id={"seg": j}, device_id_type=MESH,
        )

    def m_relay(j):
        other = seg + 1 - 2 * lax.rem(seg, 2)
        return pltpu.make_async_remote_copy(
            src_ref=mp.at[j], dst_ref=mp.at[j], send_sem=m_pass.at[j], recv_sem=m_recv.at[j],
            device_id={"seg": other}, device_id_type=MESH,
        )

    def m_direct(j):
        return (j < seg) & (lax.rem(seg + j, 2) == 0)

    def v_copy(t, source, side):
        other = sec - 1 if side == 0 else sec + 1
        return pltpu.make_async_remote_copy(
            src_ref=source, dst_ref=vh.at[t, 1 - side], send_sem=v_send.at[t, side],
            recv_sem=v_recv.at[t, 1 - side], device_id={"sec": other}, device_id_type=MESH,
        )

    def v_arrival(t, side):
        other = sec - 1 if side == 0 else sec + 1
        return pltpu.make_async_remote_copy(
            src_ref=vs.at[0, 0], dst_ref=vh.at[t, side], send_sem=v_send.at[t, side],
            recv_sem=v_recv.at[t, side], device_id={"sec": other}, device_id_type=MESH,
        )

    def r_copies(side):
        other = sec - 1 if side == 0 else sec + 1
        q, shift = (0, 1) if side == 0 else (blocks - 1, -1)
        return [
            pltpu.make_async_remote_copy(
                src_ref=right.at[0, w, q], dst_ref=rhalo.at[1 - side, i], send_sem=r_send.at[side, i],
                recv_sem=r_recv.at[1 - side, i], device_id={"sec": other}, device_id_type=MESH,
            )
            for i, w in enumerate(groups[shift])
        ]

    def r_arrivals(side):
        other = sec - 1 if side == 0 else sec + 1
        shift = -1 if side == 0 else 1
        return [
            pltpu.make_async_remote_copy(
                src_ref=right.at[0, w, 0], dst_ref=rhalo.at[side, i], send_sem=r_send.at[side, i],
                recv_sem=r_recv.at[side, i], device_id={"sec": other}, device_id_type=MESH,
            )
            for i, w in enumerate(groups[shift])
        ]

    def s_copy(stage, d):
        return pltpu.make_async_remote_copy(
            src_ref=red.at[stage, sec], dst_ref=red.at[stage, sec], send_sem=s_send.at[stage, d],
            recv_sem=s_recv.at[stage, sec], device_id={"sec": lax.rem(sec + d, n_sec)}, device_id_type=MESH,
        )

    def s_arrival(stage, d):
        other = lax.rem(sec + d, n_sec)
        return pltpu.make_async_remote_copy(
            src_ref=red.at[stage, sec], dst_ref=red.at[stage, other], send_sem=s_send.at[stage, d],
            recv_sem=s_recv.at[stage, other], device_id={"sec": other}, device_id_type=MESH,
        )

    for side, there in ((0, has_low), (1, has_high)):
        q = 0 if side == 0 else blocks - 1
        @pl.when(there)
        def _():
            v_copy(0, theta.at[0, q], side).start()
            for copy in r_copies(side):
                copy.start()

        @pl.when(jnp.logical_not(there))
        def _():
            rhalo[side] = jnp.zeros_like(rhalo[side])
            for t in range(ITERS):
                vh[t, side] = jnp.zeros_like(vh[t, side])

    def m_goes(d):
        return lax.rem(seg, 2) == 0 if d == 1 else seg + d < n_seg

    m_ways = [1] + list(range(2, n_seg, 2))
    for d in reversed(m_ways):
        @pl.when(m_goes(d))
        def _():
            m_copy(d).start()

    loads[0].wait()
    for q in range(blocks):
        for w in range(terms):
            l2[q, row[w] : row[w] + n, :] = wide(lf[w, q] * mask[q, w].astype(F32))
    loads[1].wait()
    for q in range(blocks):
        for d in (-1, 0, 1):
            if 0 <= q + d < blocks:
                for w in groups[d]:
                    r2[q, row[w] : row[w] + n, :] = wide(rt[w, q + d])
    loads[2].wait()

    for j in range(n_seg - 2):
        @pl.when(m_direct(j))
        def _():
            m_arrival(j).wait_recv()
            m_relay(j).start()

    @pl.when(seg == 0)
    def _():
        here = lax.broadcasted_iota(jnp.int32, (n, n), 0)
        across = lax.broadcasted_iota(jnp.int32, (n, n), 1)
        for q in range(blocks):
            amat[q] = (here == across).astype(F32)

    for j in range(n_seg - 1):
        @pl.when((j < seg) & jnp.logical_not(m_direct(j)))
        def _():
            m_arrival(j).wait_recv()

        @pl.when(j < seg)
        def _():
            for q in range(blocks):
                if j == 0:
                    amat[q] = mp[0, q]
                else:
                    amat[q] = halves(dot(wide(amat[q]), twice(mp[j, q])))

    for q in range(blocks):
        a = amat[q]
        turned = wide(a.T)
        doubled = twice(a)
        for d in (-1, 0, 1):
            for w in groups[d]:
                part = halves(dot(l2[q, row[w] : row[w] + n, :], doubled))
                l2[q, row[w] : row[w] + n, :] = wide(halves(dot(turned, twice(part))))

    def contribution(q, d, vector2):
        size = len(groups[d]) * n
        x = halves(dot(l2[q, start[d] : start[d] + size, :], vector2))
        x = jnp.concatenate([x[i * n : (i + 1) * n] for i in range(len(groups[d]))], axis=1)
        x = jnp.concatenate(split(x), axis=0)
        y = halves(dot(x, r2[q, start[d] : start[d] + size, :]))
        return y[:n] + y[n:]

    cells = n_sec * blocks * n * n

    def whole(stage):
        total = red[stage, 0]
        for other in range(1, n_sec):
            total = total + red[stage, other]
        first = jnp.sum(total[0], keepdims=True)
        second = jnp.sum(total[1], keepdims=True)
        return first / cells, second / cells

    def step(t, _):
        own = [twice(vs[t, q]) for q in range(blocks)]
        image = []
        for q in range(blocks):
            total = None
            for d in (-1, 0, 1):
                if 0 <= q + d < blocks:
                    y = contribution(q, d, own[q + d])
                    total = y if total is None else total + y
            vs[t + 1, q] = total

        @pl.when(t == ITERS - 1)
        def _():
            for d in range(1, n_sec):
                s_arrival(0, d).wait_recv()
            m1, m2 = whole(0)
            s1 = lax.rsqrt(m1 + EPS)
            scale[...] = jnp.broadcast_to(s1 * lax.rsqrt(s1 * s1 * m2 + EPS), scale.shape)

        sides = ((0, has_low, 0, -1), (1, has_high, blocks - 1, 1))

        @pl.when(t == 0)
        def _():
            for side, there, q, d in sides:
                @pl.when(there)
                def _():
                    for copy in r_arrivals(side):
                        copy.wait_recv()

            for side, there, q, d in sides:
                for i, w in enumerate(groups[d]):
                    r2[q, row[w] : row[w] + n, :] = wide(rhalo[side, i])

        for side, there, q, d in sides:
            @pl.when(there)
            def _():
                v_arrival(t, side).wait_recv()

        crossed = [contribution(q, d, twice(vh[t, side])) for side, _, q, d in sides]
        for side, there, q, d in sides:
            vs[t + 1, q] = vs[t + 1, q] + crossed[side]
        for side, there, q, d in sides:
            @pl.when(there & (t < ITERS - 1))
            def _():
                v_copy(t + 1, vs.at[t + 1, q], side).start()

        @pl.when(t < ITERS - 1)
        def _():
            total = squares(vs[t + 1, 0])
            for q in range(1, blocks):
                total = total + squares(vs[t + 1, q])
            red[t // 2, sec, t % 2] = total

        @pl.when(t == 1)
        def _():
            for d in range(1, n_sec):
                s_copy(0, d).start()

        return 0

    lax.fori_loop(0, ITERS, step, 0)

    s12 = scale[0:1, :]
    last = [vs[ITERS, q] * s12 for q in range(blocks)]
    total = squares(last[0])
    for q in range(1, blocks):
        total = total + squares(last[q])
    red[1, sec, 1] = total
    for d in range(1, n_sec):
        s_copy(1, d).start()

    here = lax.broadcasted_iota(jnp.int32, (n, n), 0)
    across = lax.broadcasted_iota(jnp.int32, (n, n), 1)
    for q in range(blocks):
        theta_out[0, q] = last[q]
        kept = ((here < ranks[0, q]) & (across < ranks[0, q])).astype(F32)
        density[0, q] = halves(dot(wide(last[q]), twice(last[q].T))) * kept

    for d in range(1, n_sec):
        s_arrival(1, d).wait_recv()
    m3, m4 = whole(1)
    s3 = lax.rsqrt(s12 * s12 * m3 + EPS)
    s34 = s3 * lax.rsqrt(s3 * s3 * m4 + EPS)
    for q in range(blocks):
        theta_out[0, q] = theta_out[0, q] * s34
        density[0, q] = density[0, q] * (s34 * s34 / n)

    for d in m_ways:
        @pl.when(m_goes(d))
        def _():
            m_copy(d).wait_send()
    for j in range(n_seg - 2):
        @pl.when(m_direct(j))
        def _():
            m_relay(j).wait_send()
    for side, there in ((0, has_low), (1, has_high)):
        q = 0 if side == 0 else blocks - 1
        @pl.when(there)
        def _():
            v_copy(0, theta.at[0, q], side).wait_send()
            for t in range(1, ITERS):
                v_copy(t, vs.at[t, q], side).wait_send()
            for copy in r_copies(side):
                copy.wait_send()
    for stage in range(2):
        for d in range(1, n_sec):
            s_copy(stage, d).wait_send()


def place(theta, density, theta_out, density_out, held, sem):
    arrays = ((theta, theta_out), (density, density_out))
    arrivals = [pltpu.make_async_copy(a, held.at[i], sem.at[0, i]) for i, (a, _) in enumerate(arrays)]
    departures = [pltpu.make_async_copy(held.at[i], b, sem.at[1, i]) for i, (_, b) in enumerate(arrays)]
    for copy in arrivals:
        copy.start()
    for arrival, departure in zip(arrivals, departures):
        arrival.wait()
        departure.start()
    for copy in departures:
        copy.wait()


def per_device(n_seg, n_sec, theta_in, left_env, site_maps, right_env, mpo_mask, ranks):
    terms, blocks, n, _ = left_env.shape
    groups = {d: [w for w in range(terms) if w % 3 - 1 == d] for d in (-1, 0, 1)}
    most = max(len(g) for g in groups.values())
    block = (n, n)
    anywhere = pl.BlockSpec(memory_space=pl.ANY)
    scalars = pl.BlockSpec(memory_space=pltpu.SMEM)
    vmem = pl.BlockSpec(memory_space=pltpu.VMEM)
    out = jax.ShapeDtypeStruct(theta_in.shape, F32)
    dma = pltpu.SemaphoreType.DMA
    results = pl.pallas_call(
        functools.partial(kernel, n_seg, n_sec, groups),
        out_shape=(out, out),
        in_specs=[anywhere, anywhere, anywhere, anywhere, scalars, scalars],
        out_specs=(vmem, vmem),
        scratch_shapes=[
            pltpu.VMEM((terms, blocks) + block, F32),
            pltpu.VMEM((terms, blocks) + block, F32),
            pltpu.VMEM((n_seg, blocks) + block, F32),
            pltpu.VMEM((blocks,) + block, F32),
            pltpu.VMEM((2, most) + block, F32),
            pltpu.VMEM((ITERS, 2) + block, F32),
            pltpu.VMEM((ITERS + 1, blocks) + block, F32),
            pltpu.VMEM((blocks, terms * n, 2 * n), BF16),
            pltpu.VMEM((blocks, terms * n, 2 * n), BF16),
            pltpu.VMEM((2, n_sec, 2, 8, n), F32),
            pltpu.VMEM((8, n), F32),
            dma((3,)),
            dma((n_seg,)),
            dma((n_seg,)),
            dma((n_seg,)),
            dma((2, most)),
            dma((2, most)),
            dma((ITERS, 2)),
            dma((ITERS, 2)),
            dma((2, n_sec)),
            dma((2, n_sec)),
        ],
        compiler_params=pltpu.CompilerParams(
            collective_id=0, has_side_effects=True
        ),
        cost_estimate=pl.CostEstimate(flops=2 * n**3 * 4 * 200, bytes_accessed=4 * n * n * 60, transcendentals=0),
    )(theta_in, left_env, site_maps, right_env, mpo_mask.T, ranks)
    return pl.pallas_call(
        place,
        out_shape=(out, out),
        in_specs=[anywhere, anywhere],
        out_specs=(anywhere, anywhere),
        scratch_shapes=[pltpu.VMEM((2,) + theta_in.shape, F32), dma((2, 2))],
    )(*results)


def solution(mesh):
    n_seg, n_sec = mesh.shape["seg"], mesh.shape["sec"]
    return jax.shard_map(
        functools.partial(per_device, n_seg, n_sec),
        mesh=mesh,
        in_specs=(
            P("seg", "sec", None, None),
            P(None, "sec", None, None),
            P("seg", "sec", None, None),
            P("seg", None, "sec", None, None),
            P(None, "sec"),
            P("seg", "sec"),
        ),
        out_specs=(P("seg", "sec", None, None), P("seg", "sec", None, None)),
        check_vma=False,
    )
```
